32 devices in a mesh: gx: 4 (over y, core), gy: 4 (over z), src: 2 (over x).
Axes of the slice: x: 2, y: 2, z: 4, core: 2. Of those that a mesh axis runs over, the one named last changes fastest.
Arguments:
- conductivity: float32 [8, 32, 128], P('gx', 'gy'), may hold values from 0.3 to 3
- electrodes: int32 [128, 2], replicated, may hold values from 0 to 32767
- pair_order: int32 [128], P('src'), may hold values from 0 to 127, each once
- initial_fields: float32 [128, 8, 32, 128], P('src', 'gx', 'gy'), as said below
- adjoint_fields: float32 [128, 8, 32, 128], P('src', 'gx', 'gy'), may hold values from -6 to 6
Outputs:
- potentials: float32 [128, 8, 32, 128], P('src', 'gx', 'gy')
- gradient: float32 [8, 32, 128], P('gx', 'gy', 'src')
The draws below stay inside these ranges and needn't reach their ends.
Inputs may be any that keep to these rules, and one draw needn't show every extreme that they name: `electrodes`: flat cell index (x * 32 + y) * 128 + z. `pair_order`: each pair appears once. `initial_fields`: every entry lies within 6 / sqrt(32768) in magnitude.
All inputs are finite; a program needn't handle non-finite values.
Results may differ from the reference program's by a relative error of at most 0.00029.
Values sent between devices are 32-bit elements; how exact they have to be, the bound alone decides.
A program may use at most 64 MiB of HBM per device.

```python
import math
import jax
import jax.numpy as jnp
from jax import lax

COLS = 64
ITERS = 2
NX = 8
NY = 32
NZ = 128
PAIRS = 128
N_SRC = 2


def draw_initial_fields(key, part):
    spread = 1.0 / math.sqrt(NX * NY * NZ)
    values = jnp.clip(jax.random.normal(key, (PAIRS, NX, NY, NZ), jnp.float32), -6.0, 6.0)
    return (values * spread).astype(jnp.float32)


def plant(array, rng, smallest, top_value):
    index_at = [jax.random.randint(jax.random.fold_in(rng, axis), (), 0, length) for axis, length in enumerate(array.shape)]
    main_axis = array.shape.index(max(array.shape))
    neighbour = index_at[:main_axis] + [(index_at[main_axis] + 1) % array.shape[main_axis]] + index_at[main_axis + 1:]
    return array.at[tuple(index_at)].set(smallest).at[tuple(neighbour)].set(top_value)


def shard_levels(stream_key, dims, shards, smallest, largest):
    loudness, own = 1.0, jax.random.fold_in(stream_key, 6)
    for dim, blocks in shards:
        steps = jnp.exp(jax.random.uniform(jax.random.fold_in(own, dim), (blocks,), jnp.float32, smallest / len(shards), largest / len(shards)))
        loudness = loudness * jnp.repeat(steps, dims[dim] // blocks).reshape([-1 if axis == dim else 1 for axis in range(len(dims))])
    return loudness


def normal_values(own_key, dims, scale, limit, cuts=(), kind=jnp.bfloat16):
    drawn = scale * jax.random.normal(own_key, dims, jnp.float32)
    if cuts:
        drawn = drawn * shard_levels(own_key, dims, cuts, -0.22, 0.18)
    return jnp.clip(drawn, -limit, limit).astype(kind)


def setup_inputs(seed: int = 0) -> dict:
    key_of = jax.random.split(jax.random.key(seed), 6)
    conductivity = jnp.clip(jnp.exp(math.log(3.0) - 2.3025851 * jax.random.uniform(key_of[0], (NX, NY, NZ), jnp.float32) ** shard_levels(key_of[0], (NX, NY, NZ), ((0, 4), (1, 4)), -0.2, 0.2)), 0.3, 3.0)
    electrodes = plant(jax.random.randint(key_of[1], (PAIRS, 2), 0, NX * NY * NZ), jax.random.fold_in(key_of[1], 1), 0, (NX * NY * NZ) - 1).astype(jnp.int32)
    pair_order = jax.random.permutation(key_of[2], PAIRS).astype(jnp.int32)
    initial_fields = draw_initial_fields(jax.random.fold_in(key_of[5], 71), 0)
    adjoint_fields = normal_values(key_of[4], (PAIRS, NX, NY, NZ), 1.0, 6.0, ((0, 2), (1, 4), (2, 4)), jnp.float32)
    return dict(conductivity=conductivity, electrodes=electrodes, pair_order=pair_order, initial_fields=initial_fields, adjoint_fields=adjoint_fields)


INJECT = 4.0

def conductances(sigma):
    full = jnp.pad(sigma, 1)
    cond_x = 0.5 * (full[1:, 1:-1, 1:-1] + full[:-1, 1:-1, 1:-1])
    cond_y = 0.5 * (full[1:-1, 1:, 1:-1] + full[1:-1, :-1, 1:-1])
    cond_z = 0.5 * (full[1:-1, 1:-1, 1:] + full[1:-1, 1:-1, :-1])
    return (cond_x, cond_y, cond_z)

def operator(field, conds):
    full = jnp.pad(field, ((0, 0), (1, 1), (1, 1), (1, 1)))
    flux_x = conds[0] * (full[:, 1:, 1:-1, 1:-1] - full[:, :-1, 1:-1, 1:-1])
    flux_y = conds[1] * (full[:, 1:-1, 1:, 1:-1] - full[:, 1:-1, :-1, 1:-1])
    flux_z = conds[2] * (full[:, 1:-1, 1:-1, 1:] - full[:, 1:-1, 1:-1, :-1])
    return flux_x[:, :-1] - flux_x[:, 1:] + (flux_y[:, :, :-1] - flux_y[:, :, 1:]) + (flux_z[..., :-1] - flux_z[..., 1:])

def gram_of(left, right):
    return jnp.einsum('axyz,bxyz->ab', left, right, precision=lax.Precision.HIGHEST)

def combine_cols(field, matrix):
    return jnp.einsum('axyz,ab->bxyz', field, matrix, precision=lax.Precision.HIGHEST)

def posdef_solve(matrix, right):
    lower = jnp.linalg.cholesky(matrix)
    middle = lax.linalg.triangular_solve(lower, right, left_side=True, lower=True)
    return lax.linalg.triangular_solve(lower, middle, left_side=True, lower=True, transpose_a=True)

def one_hot(cells, count):
    return (cells[:, None] == jnp.arange(count, dtype=jnp.int32)[None, :]).astype(jnp.float32)

def point_source(flat):
    xs = flat // (NY * NZ)
    ys = flat // NZ % NY
    zs = flat % NZ
    return jnp.einsum('cx,cy,cz->cxyz', one_hot(xs, NX), one_hot(ys, NY), one_hot(zs, NZ))

def reference(conductivity, electrodes, pair_order, initial_fields, adjoint_fields):
    conds = conductances(conductivity)
    results = []
    gradient = jnp.zeros((NX, NY, NZ), jnp.float32)
    for group_index in range(N_SRC):
        first = group_index * COLS
        picked = electrodes[pair_order[first:first + COLS]]
        right = INJECT * (point_source(picked[:, 0]) - point_source(picked[:, 1]))
        iterate = initial_fields[first:first + COLS]
        adjoint = adjoint_fields[first:first + COLS]
        residual = right - operator(iterate, conds)
        direction = residual
        res_gram = gram_of(residual, residual)
        for iteration in range(ITERS):
            image = operator(direction, conds)
            curv_gram = gram_of(direction, image)
            step_mat = posdef_solve(curv_gram, res_gram)
            iterate = iterate + combine_cols(direction, step_mat)
            residual = residual - combine_cols(image, step_mat)
            if iteration + 1 < ITERS:
                new_gram = gram_of(residual, residual)
                turn_mat = posdef_solve(res_gram, new_gram)
                direction = residual + combine_cols(direction, turn_mat)
                res_gram = new_gram
        results.append(iterate)
        fu = jnp.pad(iterate, ((0, 0), (1, 1), (1, 1), (1, 1)))
        fl = jnp.pad(adjoint, ((0, 0), (1, 1), (1, 1), (1, 1)))
        term_x = jnp.sum((fu[:, 1:, 1:-1, 1:-1] - fu[:, :-1, 1:-1, 1:-1]) * (fl[:, 1:, 1:-1, 1:-1] - fl[:, :-1, 1:-1, 1:-1]), axis=0)
        term_y = jnp.sum((fu[:, 1:-1, 1:, 1:-1] - fu[:, 1:-1, :-1, 1:-1]) * (fl[:, 1:-1, 1:, 1:-1] - fl[:, 1:-1, :-1, 1:-1]), axis=0)
        term_z = jnp.sum((fu[:, 1:-1, 1:-1, 1:] - fu[:, 1:-1, 1:-1, :-1]) * (fl[:, 1:-1, 1:-1, 1:] - fl[:, 1:-1, 1:-1, :-1]), axis=0)
        gradient = gradient + -0.5 / COLS * (term_x[:-1] + term_x[1:] + term_y[:, :-1] + term_y[:, 1:] + term_z[..., :-1] + term_z[..., 1:])
    return (jnp.concatenate(results, axis=0), gradient)
```

```python
import functools

import jax
import jax.numpy as jnp
from jax import lax
from jax.experimental import pallas as pl
from jax.experimental.pallas import tpu as pltpu
from jax.sharding import PartitionSpec as P

MESH = pl.DeviceIdType.MESH
INJECT = 4.0
F32 = jnp.float32
BF16 = jnp.bfloat16
HI = lax.Precision.HIGHEST


def split(x):
    hi = x.astype(BF16)
    return hi, (x - hi.astype(F32)).astype(BF16)


def nt(a, b):
    return lax.dot_general(a, b, (((1,), (1,)), ((), ())), preferred_element_type=F32)


def eliminate(lead, rest, off):
    row = lax.broadcasted_iota(jnp.int32, (8, 128), 0)
    count = len(lead)
    wide = len(rest) > 0

    def panel(_, carry):
        lead, rest = list(carry[0]), list(carry[1])
        cols = [
            [jnp.broadcast_to(tile[:, off + j : off + j + 1], (8, 128)) for tile in lead]
            for j in range(8)
        ]
        for j in range(8):
            col = cols[j]
            inv = 1.0 / jnp.broadcast_to(col[0][j : j + 1], (8, 128))

            def sweep(tiles):
                pivot = jnp.broadcast_to(tiles[0][j : j + 1], (8, 128)) * inv
                first = jnp.where(row == j, pivot, tiles[0] - col[0] * pivot)
                return [first] + [tiles[t] - col[t] * pivot for t in range(1, count)]

            for later in range(j + 1, 8):
                cols[later] = sweep(cols[later])
            lead = sweep(lead)
            if wide:
                rest = sweep(rest)
        lead = [pltpu.roll(tile, 120, 1) for tile in lead]
        lead = lead[1:] + lead[:1]
        if wide:
            rest = rest[1:] + rest[:1]
        return tuple(lead), tuple(rest)

    lead, rest = lax.fori_loop(0, count, panel, (tuple(lead), tuple(rest)))
    return jnp.concatenate(lead, axis=0), (jnp.concatenate(rest, axis=0) if wide else None)


def tiles_of(x):
    return [x[8 * t : 8 * t + 8] for t in range(x.shape[0] // 8)]


def kernel(
    sizes, x_in, adj_in, picked, x_out, grad_out,
    fx, fr, fq, fl, fs, cond, gbuf, r1, r2, gfin, gl, gr,
    send, recv, local, s1, v1, s2, v2, s3, v3, s4, v4,
):
    ngx, ngy, nsrc, cx, cy, cols = sizes
    gx, gy, src = lax.axis_index("gx"), lax.axis_index("gy"), lax.axis_index("src")

    def peer(axis, index):
        return {"gx": (index, gy, src), "gy": (gx, index, src), "src": (gx, gy, index)}[axis]

    barrier = pltpu.get_barrier_semaphore()
    groups = (("gx", gx, ngx), ("gy", gy, ngy), ("src", src, nsrc))
    for axis, me, count in groups:
        for k in range(1, count):
            pl.semaphore_signal(
                barrier, inc=1, device_id=peer(axis, lax.rem(me + k, count)), device_id_type=MESH
            )
    pl.semaphore_wait(barrier, ngx + ngy + nsrc - 3)

    low_x = (0, slice(1, cy + 1))
    inner = (slice(1, cx + 1), slice(1, cy + 1))

    def exchange(step, ref, buf, base):
        ys = pl.ds(base, cy)
        xs = pl.ds(base, cx)
        hy, hx = pl.ds(1, cy), pl.ds(1, cx)
        moves = (
            (gx > 0, gx < ngx - 1, ref.at[base, ys], buf.at[cx + 1, hy], ("gx", gx - 1)),
            (gx < ngx - 1, gx > 0, ref.at[base + cx - 1, ys], buf.at[0, hy], ("gx", gx + 1)),
            (gy > 0, gy < ngy - 1, ref.at[xs, base], buf.at[hx, cy + 1], ("gy", gy - 1)),
            (gy < ngy - 1, gy > 0, ref.at[xs, base + cy - 1], buf.at[hx, 0], ("gy", gy + 1)),
        )
        made = []
        for n, (sends, gets, source, target, (axis, index)) in enumerate(moves):
            limit = ngx if axis == "gx" else ngy
            index = jnp.clip(index, 0, limit - 1)
            copy = pltpu.make_async_remote_copy(
                src_ref=source, dst_ref=target, send_sem=send.at[step, n],
                recv_sem=recv.at[step, n], device_id=peer(axis, index), device_id_type=MESH,
            )
            made.append((sends, gets, copy, target))

            @pl.when(sends)
            def _():
                copy.start()

        def arrive():
            for sends, gets, copy, target in made:
                @pl.when(gets)
                def _():
                    copy.wait_recv()

                @pl.when(jnp.logical_not(gets))
                def _():
                    target[...] = jnp.zeros(target.shape, F32)

        def leave():
            for sends, gets, copy, target in made:
                @pl.when(sends)
                def _():
                    copy.wait_send()

        return arrive, leave

    arrive0, leave0 = exchange(0, x_in, fx, 0)
    load_x = pltpu.make_async_copy(x_in, fx.at[pl.ds(1, cx), pl.ds(1, cy)], local.at[0])
    load_x.start()
    load_l = pltpu.make_async_copy(adj_in, fl.at[pl.ds(1, cx), pl.ds(1, cy)], local.at[1])
    load_l.start()
    load_x.wait()
    arrive0()

    lane = lax.broadcasted_iota(jnp.int32, (8, 128), 1)

    def each_cell(body):
        def step(i, carry):
            body(i // cy, lax.rem(i, cy))
            return carry

        lax.fori_loop(0, cx * cy, step, 0)

    def conductance(x, y):
        def sig(i, j):
            return fx[i, j, cols:, :]

        mid = sig(x + 1, y + 1)
        parts = [
            0.5 * (mid + sig(x, y + 1)),
            0.5 * (mid + sig(x + 2, y + 1)),
            0.5 * (mid + sig(x + 1, y)),
            0.5 * (mid + sig(x + 1, y + 2)),
            0.5 * (mid + jnp.where(lane == 0, 0.0, pltpu.roll(mid, 1, 1))),
            0.5 * (mid + jnp.where(lane == 127, 0.0, pltpu.roll(mid, 127, 1))),
        ]
        total = parts[0] + parts[1] + (parts[2] + parts[3]) + (parts[4] + parts[5])
        parts[4] = jnp.where(lane == 0, 0.0, parts[4])
        parts[5] = jnp.where(lane == 127, 0.0, parts[5])
        for n, part in enumerate(parts + [total]):
            cond[x, y, n] = part

    def image(buf, x, y):
        def at(i, j):
            return buf[i, j, :cols, :].reshape(cols // 8, 8, 128)

        mid = at(x + 1, y + 1)
        flat = mid.reshape(cols, 128)
        down = pltpu.roll(flat, 1, 1).reshape(cols // 8, 8, 128)
        up = pltpu.roll(flat, 127, 1).reshape(cols // 8, 8, 128)
        c = [cond[x, y, n][None] for n in range(7)]
        out = c[6] * mid - (
            c[0] * at(x, y + 1) + c[1] * at(x + 2, y + 1)
            + (c[2] * at(x + 1, y) + c[3] * at(x + 1, y + 2))
            + (c[4] * down + c[5] * up)
        )
        return out.reshape(cols, 128)

    each_cell(conductance)

    lane_c = lax.broadcasted_iota(jnp.int32, (cols, 128), 1)

    def residual(x, y):
        base = ((gx * cx + x) * (ngy * cy) + gy * cy + y) * 128
        right = jnp.where(picked[0] - base == lane_c, INJECT, 0.0) - jnp.where(
            picked[1] - base == lane_c, INJECT, 0.0
        )
        fr[x + 1, y + 1] = right - image(fx, x, y)

    each_cell(residual)
    arrive1, leave1 = exchange(1, fr, fr, 1)
    arrive1()

    def first(x, y):
        fq[x + 1, y + 1] = image(fr, x, y)

    each_cell(first)
    arrive2, leave2 = exchange(2, fq, fq, 1)
    load_l.wait()
    arrive3, leave3 = exchange(3, fl, fl, 1)
    arrive2()

    def second(x, y):
        fs[x, y] = image(fq, x, y)

    each_cell(second)

    def gram(i, carry):
        x, y = i // (cy // 2), 2 * lax.rem(i, cy // 2)

        def pair(buf, o):
            return split(jnp.concatenate([buf[x + o, y + o], buf[x + o, y + o + 1]], axis=1))

        (rh, rl), (qh, ql), (sh, sl) = pair(fr, 1), pair(fq, 1), pair(fs, 0)
        rqh, rql = jnp.concatenate([rh, qh], axis=0), jnp.concatenate([rl, ql], axis=0)
        qsh, qsl = jnp.concatenate([qh, sh], axis=0), jnp.concatenate([ql, sl], axis=0)
        a = nt(rh, rqh) + (nt(rh, rql) + nt(rl, rqh))
        b = nt(qh, qsh) + (nt(qh, qsl) + nt(ql, qsh))
        return carry[0] + a, carry[1] + b

    zero = jnp.zeros((cols, 2 * cols), F32)
    ga, gb = lax.fori_loop(0, cx * cy // 2, gram, (zero, zero))
    rows = 2 * cols // ngx
    both = jnp.concatenate([ga, gb], axis=0)
    gbuf[...] = both.reshape(ngx, rows, 2 * cols)

    made = []
    for k in range(1, ngx):
        to = lax.rem(gx + k, ngx)
        copy = pltpu.make_async_remote_copy(
            src_ref=gbuf.at[to], dst_ref=r1.at[k - 1], send_sem=s1.at[k - 1],
            recv_sem=v1.at[k - 1], device_id=peer("gx", to), device_id_type=MESH,
        )
        copy.start()
        made.append(copy)
    share = gbuf[gx]
    for k, copy in enumerate(made):
        copy.wait_recv()
        share = share + r1[k]
    r2[gy] = share
    late = list(made)
    made = []
    for k in range(1, ngy):
        to = lax.rem(gy + k, ngy)
        copy = pltpu.make_async_remote_copy(
            src_ref=r2.at[gy], dst_ref=r2.at[gy], send_sem=s2.at[k - 1],
            recv_sem=v2.at[k - 1], device_id=peer("gy", to), device_id_type=MESH,
        )
        copy.start()
        made.append(copy)
    late += made
    for copy in made:
        copy.wait_recv()
    total = r2[0]
    for k in range(1, ngy):
        total = total + r2[k]
    gfin[gx] = total
    made = []
    for k in range(1, ngx):
        to = lax.rem(gx + k, ngx)
        copy = pltpu.make_async_remote_copy(
            src_ref=gfin.at[gx], dst_ref=gfin.at[gx], send_sem=s3.at[k - 1],
            recv_sem=v3.at[k - 1], device_id=peer("gx", to), device_id_type=MESH,
        )
        copy.start()
        made.append(copy)
    late += made
    for copy in made:
        copy.wait_recv()

    whole = gfin[...].reshape(2 * cols, 2 * cols)
    top, low = whole[:cols], whole[cols:]
    lead, rest = eliminate(tiles_of(top), tiles_of(low), cols)
    alpha = lead[:, cols:]
    inv2 = rest[:, :cols]
    g2, g3, g1 = low[:, :cols], low[:, cols:], top[:, cols:]
    prod = jnp.dot(
        g2, jnp.concatenate([alpha, inv2], axis=1), precision=HI, preferred_element_type=F32
    )
    system = jnp.concatenate([g1, g3], axis=1) - prod
    lead, _ = eliminate(tiles_of(system), [], cols)
    c1 = lead[:, cols:]
    c0 = alpha - jnp.dot(inv2, c1, precision=HI, preferred_element_type=F32)
    stacked = jnp.concatenate([c0, c1], axis=0)
    stacked = jnp.concatenate([stacked, jnp.zeros_like(stacked)], axis=1).T[:cols]
    ch, cl = split(stacked)
    factors = jnp.concatenate(
        [
            jnp.concatenate([ch, ch], axis=1),
            jnp.concatenate([cl, jnp.zeros_like(cl)], axis=1),
        ],
        axis=0,
    )

    def advance(x, y):
        def pair(buf):
            return jnp.concatenate([buf[x, y], buf[x, y + 1]], axis=1)

        hi, lo = split(jnp.concatenate([pair(fr), pair(fq)], axis=0))
        out = jnp.dot(factors, jnp.concatenate([hi, lo], axis=0), preferred_element_type=F32)
        out = out[:cols] + out[cols:]
        fx[x, y, :cols, :] = fx[x, y, :cols, :] + out[:, :128]
        fx[x, y + 1, :cols, :] = fx[x, y + 1, :cols, :] + out[:, 128:]

    def inner_rows(i, carry):
        for x in range(1, cx + 1):
            advance(x, 2 * i)
        return carry

    def outer_rows(i, carry):
        for x in (0, cx + 1):
            advance(x, 2 * i + 1)
        return carry

    lax.fori_loop(0, (cy + 2) // 2, inner_rows, 0)
    store = pltpu.make_async_copy(
        fx.at[pl.ds(1, cx), pl.ds(1, cy), pl.ds(0, cols)], x_out, local.at[2]
    )
    store.start()
    lax.fori_loop(0, cy // 2, outer_rows, 0)

    arrive3()

    def field(i, ys):
        return fx[i, ys, :cols, :], fl[i, ys, :, :]

    mid_y = slice(1, cy + 1)
    term_x = []
    for i in range(cx + 1):
        (u0, l0), (u1, l1) = field(i, mid_y), field(i + 1, mid_y)
        term_x.append(jnp.sum((u1 - u0) * (l1 - l0), axis=1))
    lane_y = lax.broadcasted_iota(jnp.int32, (cy, 128), 1)
    for i in range(cx):
        (u0, l0), (u1, l1) = field(i + 1, slice(0, cy + 1)), field(i + 1, slice(1, cy + 2))
        term_y = jnp.sum((u1 - u0) * (l1 - l0), axis=1)
        u, l = field(i + 1, mid_y)
        u, l = u.reshape(cy * cols, 128), l.reshape(cy * cols, 128)
        lane_f = lax.broadcasted_iota(jnp.int32, u.shape, 1)
        du = u - jnp.where(lane_f == 0, 0.0, pltpu.roll(u, 1, 1))
        dl = l - jnp.where(lane_f == 0, 0.0, pltpu.roll(l, 1, 1))
        term_z = jnp.sum((du * dl).reshape(cy, cols, 128), axis=1)
        last = jnp.sum((u * l).reshape(cy, cols, 128), axis=1)
        upper = jnp.where(lane_y == 127, last, pltpu.roll(term_z, 127, 1))
        gl[i] = (-0.5 / cols) * (
            term_x[i] + term_x[i + 1] + term_y[:-1] + term_y[1:] + term_z + upper
        )

    made = []
    for k in range(1, nsrc):
        copy = pltpu.make_async_remote_copy(
            src_ref=gl, dst_ref=gr.at[k - 1], send_sem=s4.at[k - 1], recv_sem=v4.at[k - 1],
            device_id=peer("src", lax.rem(src + k, nsrc)), device_id_type=MESH,
        )
        copy.start()
        made.append(copy)
    late += made
    summed = gl[...]
    for k, copy in enumerate(made):
        copy.wait_recv()
        summed = summed + gr[k]
    width = 128 // nsrc
    part = summed[:, :, :width]
    for k in range(1, nsrc):
        part = jnp.where(src == k, summed[:, :, k * width : (k + 1) * width], part)
    grad_out[...] = part
    store.wait()
    leave0()
    leave1()
    leave2()
    leave3()
    for copy in late:
        copy.wait_send()


def on_device(sizes, conductivity, electrodes, pair_order, initial_fields, adjoint_fields):
    ngx, ngy, nsrc = sizes
    cols, cx, cy, cz = initial_fields.shape
    pairs = jnp.arange(electrodes.shape[0], dtype=jnp.int32)
    hit = pair_order[:, None] == pairs[None, :]
    picked = jnp.sum(jnp.where(hit[None], electrodes.T[:, None, :], 0), axis=-1)
    picked = jnp.broadcast_to(picked[:, :, None], (2, cols, cz))
    x_in = jnp.concatenate(
        [
            initial_fields.transpose(1, 2, 0, 3),
            jnp.broadcast_to(conductivity[:, :, None, :], (cx, cy, 8, cz)),
        ],
        axis=2,
    )
    adj_in = adjoint_fields.transpose(1, 2, 0, 3)
    rows = 2 * cols // ngx
    dma = pltpu.SemaphoreType.DMA
    full = (cx + 2, cy + 2, cols, cz)
    x_out, grad = pl.pallas_call(
        functools.partial(kernel, (ngx, ngy, nsrc, cx, cy, cols)),
        out_shape=(
            jax.ShapeDtypeStruct((cx, cy, cols, cz), F32),
            jax.ShapeDtypeStruct((cx, cy, cz // nsrc), F32),
        ),
        in_specs=[
            pl.BlockSpec(memory_space=pl.ANY),
            pl.BlockSpec(memory_space=pl.ANY),
            pl.BlockSpec(memory_space=pltpu.VMEM),
        ],
        out_specs=(
            pl.BlockSpec(memory_space=pl.ANY),
            pl.BlockSpec(memory_space=pltpu.VMEM),
        ),
        scratch_shapes=[
            pltpu.VMEM((cx + 2, cy + 2, cols + 8, cz), F32),
            pltpu.VMEM(full, F32),
            pltpu.VMEM(full, F32),
            pltpu.VMEM(full, F32),
            pltpu.VMEM((cx, cy, cols, cz), F32),
            pltpu.VMEM((cx, cy, 7, 8, cz), F32),
            pltpu.VMEM((ngx, rows, 2 * cols), F32),
            pltpu.VMEM((ngx - 1, rows, 2 * cols), F32),
            pltpu.VMEM((ngy, rows, 2 * cols), F32),
            pltpu.VMEM((ngx, rows, 2 * cols), F32),
            pltpu.VMEM((cx, cy, cz), F32),
            pltpu.VMEM((nsrc - 1, cx, cy, cz), F32),
            dma((4, 4)), dma((4, 4)), dma((3,)),
            dma((ngx - 1,)), dma((ngx - 1,)),
            dma((ngy - 1,)), dma((ngy - 1,)),
            dma((ngx - 1,)), dma((ngx - 1,)),
            dma((nsrc - 1,)), dma((nsrc - 1,)),
        ],
        compiler_params=pltpu.CompilerParams(
            collective_id=0, has_side_effects=True, vmem_limit_bytes=32 * 1024 * 1024
        ),
        cost_estimate=pl.CostEstimate(
            flops=4 * 10**8, bytes_accessed=2 * 10**6, transcendentals=0
        ),
    )(x_in, adj_in, picked)
    return x_out.transpose(2, 0, 1, 3), grad


def solution(mesh):
    sizes = (mesh.shape["gx"], mesh.shape["gy"], mesh.shape["src"])
    field = P("src", "gx", "gy", None)
    return jax.shard_map(
        functools.partial(on_device, sizes),
        mesh=mesh,
        in_specs=(P("gx", "gy", None), P(), P("src"), field, field),
        out_specs=(field, P("gx", "gy", "src")),
        check_vma=False,
    )
```

```python
import functools

import jax
import jax.numpy as jnp
from jax import lax
from jax.experimental import pallas as pl
from jax.experimental.pallas import tpu as pltpu
from jax.sharding import PartitionSpec as P

MESH = pl.DeviceIdType.MESH
INJECT = 4.0
F32 = jnp.float32
BF16 = jnp.bfloat16
HI = lax.Precision.HIGHEST


def split(x):
    hi = x.astype(BF16)
    return hi, (x - hi.astype(F32)).astype(BF16)


def nt(a, b):
    return lax.dot_general(a, b, (((1,), (1,)), ((), ())), preferred_element_type=F32)


def eliminate(lead, rest, off, panels):
    row = lax.broadcasted_iota(jnp.int32, (8, 128), 0)
    count = len(lead)
    wide = len(rest) > 0

    def spread(tile, j):
        return jnp.broadcast_to(tile[j : j + 1], (8, 128))

    def panel(_, carry):
        lead, rest = list(carry[0]), list(carry[1])
        cols = [
            [jnp.broadcast_to(tile[:, off + j : off + j + 1], (8, 128)) for tile in lead]
            for j in range(8)
        ]
        for j in range(0, 8, 2):
            a, b = cols[j], cols[j + 1]
            a0, a1, b0, b1 = spread(a[0], j), spread(a[0], j + 1), spread(b[0], j), spread(b[0], j + 1)
            inv = 1.0 / (a0 * b1 - a1 * b0)
            i00, i01, i10, i11 = b1 * inv, b0 * inv, a1 * inv, a0 * inv

            def sweep(tiles):
                r0, r1 = spread(tiles[0], j), spread(tiles[0], j + 1)
                n0 = i00 * r0 - i01 * r1
                n1 = i11 * r1 - i10 * r0
                out = [tiles[t] - (a[t] * n0 + b[t] * n1) for t in range(count)]
                out[0] = jnp.where(row == j, n0, jnp.where(row == j + 1, n1, out[0]))
                return out

            for later in range(j + 2, 8):
                cols[later] = sweep(cols[later])
            lead = sweep(lead)
            if wide:
                rest = sweep(rest)
        lead = [pltpu.roll(tile, 120, 1) for tile in lead]
        lead = lead[1:] + lead[:1]
        if wide:
            rest = rest[1:] + rest[:1]
        return tuple(lead), tuple(rest)

    return lax.fori_loop(0, panels, panel, (tuple(lead), tuple(rest)))


def tiles_of(x):
    return [x[8 * t : 8 * t + 8] for t in range(x.shape[0] // 8)]


PARTS = 2


def kernel(
    sizes, sig_in, elec_in, order_in, x_in, adj_in, x_out, grad_out,
    fx, fr, fq, fl, fs, cond, sig, elec, order, picked,
    gbufs, r1s, r2s, gfins, gl, gr,
    send, recv, local, s1s, v1s, s2s, v2s, s3s, v3s, s4, v4,
):
    ngx, ngy, nsrc, cx, cy, cols = sizes
    gx, gy, src = lax.axis_index("gx"), lax.axis_index("gy"), lax.axis_index("src")
    half = cols // PARTS

    def peer(axis, index):
        return {"gx": (index, gy, src), "gy": (gx, index, src), "src": (gx, gy, index)}[axis]

    small = [
        pltpu.make_async_copy(sig_in, sig, local.at[0]),
        pltpu.make_async_copy(elec_in, elec, local.at[1]),
        pltpu.make_async_copy(order_in, order, local.at[2]),
    ]
    for copy in small:
        copy.start()

    def load(source, buf, low, count, sem):
        for x in range(cx):
            for y in range(cy):
                pltpu.make_async_copy(
                    source.at[pl.ds(low, count), x, y],
                    buf.at[x + 1, y + 1, pl.ds(low, count)],
                    sem,
                ).start()
        whole = buf.at[pl.ds(1, cx), pl.ds(1, cy), pl.ds(low, count)]
        return pltpu.make_async_copy(whole, whole, sem)

    loads = [load(x_in, fx, h * half, half, local.at[3 + h]) for h in range(PARTS)]

    barrier = pltpu.get_barrier_semaphore()
    groups = (("gx", gx, ngx), ("gy", gy, ngy), ("src", src, nsrc))
    for axis, me, count in groups:
        for k in range(1, count):
            pl.semaphore_signal(
                barrier, inc=1, device_id=peer(axis, lax.rem(me + k, count)), device_id_type=MESH
            )

    def exchange(step, buf, low, count):
        zs = pl.ds(low, count)
        hx, hy = pl.ds(1, cx), pl.ds(1, cy)
        moves = (
            (gx > 0, gx < ngx - 1, buf.at[1, hy, zs], buf.at[cx + 1, hy, zs], ("gx", gx - 1)),
            (gx < ngx - 1, gx > 0, buf.at[cx, hy, zs], buf.at[0, hy, zs], ("gx", gx + 1)),
            (gy > 0, gy < ngy - 1, buf.at[hx, 1, zs], buf.at[hx, cy + 1, zs], ("gy", gy - 1)),
            (gy < ngy - 1, gy > 0, buf.at[hx, cy, zs], buf.at[hx, 0, zs], ("gy", gy + 1)),
        )
        made = []
        for n, (sends, gets, source, target, (axis, index)) in enumerate(moves):
            limit = ngx if axis == "gx" else ngy
            index = jnp.clip(index, 0, limit - 1)
            copy = pltpu.make_async_remote_copy(
                src_ref=source, dst_ref=target, send_sem=send.at[step, n],
                recv_sem=recv.at[step, n], device_id=peer(axis, index), device_id_type=MESH,
            )
            made.append((sends, gets, copy, target))

            @pl.when(sends)
            def _():
                copy.start()

            @pl.when(jnp.logical_not(gets))
            def _():
                target[...] = jnp.zeros(target.shape, F32)

        def arrive():
            for sends, gets, copy, target in made:
                @pl.when(gets)
                def _():
                    copy.wait_recv()

        def leave():
            for sends, gets, copy, target in made:
                @pl.when(sends)
                def _():
                    copy.wait_send()

        leaves.append(leave)
        return arrive

    leaves = []
    for copy in small:
        copy.wait()
    for x in range(cx):
        for y in range(cy):
            fx[x + 1, y + 1, cols:, :] = jnp.broadcast_to(sig[x, y : y + 1, :], (8, 128))
    pl.semaphore_wait(barrier, ngx + ngy + nsrc - 3)
    arrive_sig = exchange(0, fx, cols, 8)
    arrive_x = []
    for h in range(PARTS):
        loads[h].wait()
        arrive_x.append(exchange(1 + h, fx, h * half, half))
    load_l = load(adj_in, fl, 0, cols, local.at[3 + PARTS])

    lane = lax.broadcasted_iota(jnp.int32, (8, 128), 1)

    pairs = elec.shape[1]
    slot = jnp.concatenate([order[...], jnp.full((1, 128 - cols), -1, jnp.int32)], axis=1)
    hit = lax.broadcasted_iota(jnp.int32, (pairs, 128), 0) == jnp.broadcast_to(slot, (pairs, 128))
    table = jnp.concatenate([elec[...].astype(F32), jnp.zeros((6, pairs), F32)], axis=0)
    cells = jnp.dot(table, hit.astype(F32), precision=HI, preferred_element_type=F32).T
    for n in range(2):
        picked[n] = jnp.broadcast_to(cells[:cols, n : n + 1], (cols, 128)).astype(jnp.int32)

    group = 4

    def each_cell(body):
        def step(i, carry):
            x, y = i // (cy // group), group * lax.rem(i, cy // group)
            for k in range(group):
                body(x, y + k)
            return carry

        lax.fori_loop(0, cx * cy // group, step, 0)

    def conductance(x, y):
        def sig_at(i, j):
            return fx[i, j, cols:, :]

        mid = sig_at(x + 1, y + 1)
        parts = [
            0.5 * (mid + sig_at(x, y + 1)),
            0.5 * (mid + sig_at(x + 2, y + 1)),
            0.5 * (mid + sig_at(x + 1, y)),
            0.5 * (mid + sig_at(x + 1, y + 2)),
            0.5 * (mid + jnp.where(lane == 0, 0.0, pltpu.roll(mid, 1, 1))),
            0.5 * (mid + jnp.where(lane == 127, 0.0, pltpu.roll(mid, 127, 1))),
        ]
        total = parts[0] + parts[1] + (parts[2] + parts[3]) + (parts[4] + parts[5])
        parts[4] = jnp.where(lane == 0, 0.0, parts[4])
        parts[5] = jnp.where(lane == 127, 0.0, parts[5])
        for n, part in enumerate(parts + [total]):
            cond[x, y, n] = part

    def image(buf, x, y, h):
        rows = slice(h * half, (h + 1) * half)

        def at(i, j):
            return buf[i, j, rows, :].reshape(half // 8, 8, 128)

        flat = buf[x + 1, y + 1, rows, :]
        mid = flat.reshape(half // 8, 8, 128)
        down = pltpu.roll(flat, 1, 1).reshape(half // 8, 8, 128)
        up = pltpu.roll(flat, 127, 1).reshape(half // 8, 8, 128)
        c = [cond[x, y, n][None] for n in range(7)]
        out = c[6] * mid - (
            c[0] * at(x, y + 1) + c[1] * at(x + 2, y + 1)
            + (c[2] * at(x + 1, y) + c[3] * at(x + 1, y + 2))
            + (c[4] * down + c[5] * up)
        )
        return out.reshape(half, 128)

    arrive_sig()
    each_cell(conductance)

    lane_c = lax.broadcasted_iota(jnp.int32, (half, 128), 1)

    arrive_r = []
    for h in range(PARTS):
        rows = slice(h * half, (h + 1) * half)

        def residual(x, y):
            base = ((gx * cx + x) * (ngy * cy) + gy * cy + y) * 128
            right = jnp.where(picked[0, rows] - base == lane_c, INJECT, 0.0) - jnp.where(
                picked[1, rows] - base == lane_c, INJECT, 0.0
            )
            fr[x + 1, y + 1, rows, :] = right - image(fx, x, y, h)

        arrive_x[h]()
        each_cell(residual)
        arrive_r.append(exchange(1 + PARTS + h, fr, h * half, half))

    arrive_q = []
    for h in range(PARTS):
        def first(x, y):
            fq[x + 1, y + 1, slice(h * half, (h + 1) * half), :] = image(fr, x, y, h)

        arrive_r[h]()
        each_cell(first)
        arrive_q.append(exchange(1 + 2 * PARTS + h, fq, h * half, half))

    load_l.wait()
    arrive_l = exchange(1 + 3 * PARTS, fl, 0, cols)

    def wide_of(buf, o, i):
        x, y = i // (cy // group), group * lax.rem(i, cy // group)
        return split(
            jnp.concatenate([buf[x + o, y + o + k] for k in range(group)], axis=1)
        )

    def times(left, right):
        return nt(left[0], right[0]) + (nt(left[0], right[1]) + nt(left[1], right[0]))

    def early(i, carry):
        r, q = wide_of(fr, 1, i), wide_of(fq, 1, i)
        rq = [jnp.concatenate([u, v], axis=0) for u, v in zip(r, q)]
        return carry[0] + times(r, rq), carry[1] + times(q, q)

    steps = cx * cy // group
    square, double = jnp.zeros((cols, cols), F32), jnp.zeros((cols, 2 * cols), F32)
    g01, g22 = lax.fori_loop(0, steps, early, (double, square))

    late = []

    def reduction(n, value):
        gbuf, r1, r2, gfin = gbufs[n], r1s[n], r2s[n], gfins[n]
        s1, v1, s2, v2, s3, v3 = s1s.at[n], v1s.at[n], s2s.at[n], v2s.at[n], s3s.at[n], v3s.at[n]
        gbuf[...] = value.reshape(gbuf.shape)

        def spread(axis, me, count, pieces, sems, waits):
            made = []
            for k in range(1, count):
                to = lax.rem(me + k, count)
                source, target = pieces(k, to)
                copy = pltpu.make_async_remote_copy(
                    src_ref=source, dst_ref=target, send_sem=sems.at[k - 1],
                    recv_sem=waits.at[k - 1], device_id=peer(axis, to), device_id_type=MESH,
                )
                copy.start()
                made.append(copy)
            late.extend(made)
            return made

        made = spread("gx", gx, ngx, lambda k, to: (gbuf.at[to], r1.at[k - 1]), s1, v1)

        def second():
            share = gbuf[gx]
            for k, copy in enumerate(made):
                copy.wait_recv()
                share = share + r1[k]
            r2[gy] = share
            made[:] = spread("gy", gy, ngy, lambda k, to: (r2.at[gy], r2.at[gy]), s2, v2)

        def third():
            for copy in made:
                copy.wait_recv()
            total = r2[0]
            for k in range(1, ngy):
                total = total + r2[k]
            gfin[gx] = total
            made[:] = spread("gx", gx, ngx, lambda k, to: (gfin.at[gx], gfin.at[gx]), s3, v3)

        def last():
            for copy in made:
                copy.wait_recv()
            return gfin[...].reshape(value.shape)

        return second, third, last

    second_a, third_a, last_a = reduction(
        0, jnp.concatenate([g01, jnp.concatenate([g22, square], axis=1)], axis=0)
    )

    for h in range(PARTS):
        def next_image(x, y):
            fs[x, y, slice(h * half, (h + 1) * half), :] = image(fq, x, y, h)

        arrive_q[h]()
        each_cell(next_image)
    second_a()

    def final(i, carry):
        return carry + times(wide_of(fq, 1, i), wide_of(fs, 0, i))

    g33 = lax.fori_loop(0, steps, final, square)
    second_b, third_b, last_b = reduction(1, jnp.concatenate([g33, square], axis=1))
    third_a()
    second_b()
    whole = last_a()
    top, low = whole[:cols], whole[cols:]
    panels = cols // 8
    state = eliminate(tiles_of(top), tiles_of(low), cols, panels // 2)
    third_b()
    lead, rest = eliminate(*state, cols, panels - panels // 2)
    lead, rest = jnp.concatenate(lead, axis=0), jnp.concatenate(rest, axis=0)
    alpha = lead[:, cols:]
    inv2 = rest[:, :cols]
    g2, g1 = low[:, :cols], top[:, cols:]
    prod = jnp.dot(
        g2, jnp.concatenate([alpha, inv2], axis=1), precision=HI, preferred_element_type=F32
    )
    g3 = last_b()[:, :cols]
    system = jnp.concatenate([g1, g3], axis=1) - prod
    lead, _ = eliminate(tiles_of(system), [], cols, panels)
    c1 = jnp.concatenate(lead, axis=0)[:, cols:]
    c0 = alpha - jnp.dot(inv2, c1, precision=HI, preferred_element_type=F32)
    stacked = jnp.concatenate([c0, c1], axis=0)
    stacked = jnp.concatenate([stacked, jnp.zeros_like(stacked)], axis=1).T[:cols]
    ch, cl = split(stacked)
    factors = jnp.concatenate(
        [
            jnp.concatenate([ch, ch], axis=1),
            jnp.concatenate([cl, jnp.zeros_like(cl)], axis=1),
        ],
        axis=0,
    )

    def advance(x, y):
        def pair(buf):
            return jnp.concatenate([buf[x, y], buf[x, y + 1]], axis=1)

        hi, lo = split(jnp.concatenate([pair(fr), pair(fq)], axis=0))
        out = jnp.dot(factors, jnp.concatenate([hi, lo], axis=0), preferred_element_type=F32)
        out = out[:cols] + out[cols:]
        fx[x, y, :cols, :] = fx[x, y, :cols, :] + out[:, :128]
        fx[x, y + 1, :cols, :] = fx[x, y + 1, :cols, :] + out[:, 128:]

    for leave in leaves:
        leave()
    for x in range(1, cx + 1):
        for y in range(0, cy + 2, 2):
            advance(x, y)
    store = pltpu.make_async_copy(
        fx.at[pl.ds(1, cx), pl.ds(1, cy), pl.ds(0, cols)], x_out, local.at[0]
    )
    store.start()
    for x in (0, cx + 1):
        for y in range(1, cy + 1, 2):
            advance(x, y)

    arrive_l()

    def field(i, ys):
        return fx[i, ys, :cols, :], fl[i, ys, :, :]

    mid_y = slice(1, cy + 1)
    term_x = []
    for i in range(cx + 1):
        (u0, l0), (u1, l1) = field(i, mid_y), field(i + 1, mid_y)
        term_x.append(jnp.sum((u1 - u0) * (l1 - l0), axis=1))
    lane_y = lax.broadcasted_iota(jnp.int32, (cy, 128), 1)
    for i in range(cx):
        (u0, l0), (u1, l1) = field(i + 1, slice(0, cy + 1)), field(i + 1, slice(1, cy + 2))
        term_y = jnp.sum((u1 - u0) * (l1 - l0), axis=1)
        u, l = field(i + 1, mid_y)
        u, l = u.reshape(cy * cols, 128), l.reshape(cy * cols, 128)
        lane_f = lax.broadcasted_iota(jnp.int32, u.shape, 1)
        du = u - jnp.where(lane_f == 0, 0.0, pltpu.roll(u, 1, 1))
        dl = l - jnp.where(lane_f == 0, 0.0, pltpu.roll(l, 1, 1))
        term_z = jnp.sum((du * dl).reshape(cy, cols, 128), axis=1)
        end = jnp.sum((u * l).reshape(cy, cols, 128), axis=1)
        upper = jnp.where(lane_y == 127, end, pltpu.roll(term_z, 127, 1))
        gl[i] = (-0.5 / cols) * (
            term_x[i] + term_x[i + 1] + term_y[:-1] + term_y[1:] + term_z + upper
        )

    made = []
    for k in range(1, nsrc):
        copy = pltpu.make_async_remote_copy(
            src_ref=gl, dst_ref=gr.at[k - 1], send_sem=s4.at[k - 1], recv_sem=v4.at[k - 1],
            device_id=peer("src", lax.rem(src + k, nsrc)), device_id_type=MESH,
        )
        copy.start()
        made.append(copy)
    late.extend(made)
    summed = gl[...]
    for k, copy in enumerate(made):
        copy.wait_recv()
        summed = summed + gr[k]
    width = 128 // nsrc
    part = summed[:, :, :width]
    for k in range(1, nsrc):
        part = jnp.where(src == k, summed[:, :, k * width : (k + 1) * width], part)
    grad_out[...] = part
    store.wait()
    for copy in late:
        copy.wait_send()


def on_device(sizes, conductivity, electrodes, pair_order, initial_fields, adjoint_fields):
    ngx, ngy, nsrc = sizes
    cols, cx, cy, cz = initial_fields.shape
    pairs = electrodes.shape[0]
    dma = pltpu.SemaphoreType.DMA
    full = (cx + 2, cy + 2, cols, cz)
    rows = (2 * cols // ngx, cols // ngx)
    steps = 2 + 3 * PARTS
    x_out, grad = pl.pallas_call(
        functools.partial(kernel, (ngx, ngy, nsrc, cx, cy, cols)),
        out_shape=(
            jax.ShapeDtypeStruct((cx, cy, cols, cz), F32),
            jax.ShapeDtypeStruct((cx, cy, cz // nsrc), F32),
        ),
        in_specs=[pl.BlockSpec(memory_space=pltpu.HBM)] * 5,
        out_specs=(
            pl.BlockSpec(memory_space=pl.ANY),
            pl.BlockSpec(memory_space=pltpu.VMEM),
        ),
        scratch_shapes=[
            pltpu.VMEM((cx + 2, cy + 2, cols + 8, cz), F32),
            pltpu.VMEM(full, F32),
            pltpu.VMEM(full, F32),
            pltpu.VMEM(full, F32),
            pltpu.VMEM((cx, cy, cols, cz), F32),
            pltpu.VMEM((cx, cy, 7, 8, cz), F32),
            pltpu.VMEM((cx, cy, cz), F32),
            pltpu.VMEM((2, pairs), jnp.int32),
            pltpu.VMEM((1, cols), jnp.int32),
            pltpu.VMEM((2, cols, cz), jnp.int32),
            [pltpu.VMEM((ngx, n, 2 * cols), F32) for n in rows],
            [pltpu.VMEM((ngx - 1, n, 2 * cols), F32) for n in rows],
            [pltpu.VMEM((ngy, n, 2 * cols), F32) for n in rows],
            [pltpu.VMEM((ngx, n, 2 * cols), F32) for n in rows],
            pltpu.VMEM((cx, cy, cz), F32),
            pltpu.VMEM((nsrc - 1, cx, cy, cz), F32),
            dma((steps, 4)), dma((steps, 4)), dma((4 + PARTS,)),
            dma((2, ngx - 1)), dma((2, ngx - 1)),
            dma((2, ngy - 1)), dma((2, ngy - 1)),
            dma((2, ngx - 1)), dma((2, ngx - 1)),
            dma((nsrc - 1,)), dma((nsrc - 1,)),
        ],
        compiler_params=pltpu.CompilerParams(
            collective_id=0, has_side_effects=True, vmem_limit_bytes=62 * 1024 * 1024
        ),
        cost_estimate=pl.CostEstimate(
            flops=4 * 10**8, bytes_accessed=2 * 10**6, transcendentals=0
        ),
    )(
        conductivity, electrodes.T, pair_order.reshape(1, cols), initial_fields, adjoint_fields
    )
    return x_out.transpose(2, 0, 1, 3), grad


def solution(mesh):
    sizes = (mesh.shape["gx"], mesh.shape["gy"], mesh.shape["src"])
    field = P("src", "gx", "gy", None)
    return jax.shard_map(
        functools.partial(on_device, sizes),
        mesh=mesh,
        in_specs=(P("gx", "gy", None), P(), P("src"), field, field),
        out_specs=(field, P("gx", "gy", "src")),
        check_vma=False,
    )
```

```python
import functools

import jax
import jax.numpy as jnp
from jax import lax
from jax.experimental import pallas as pl
from jax.experimental.pallas import tpu as pltpu
from jax.sharding import PartitionSpec as P

MESH = pl.DeviceIdType.MESH
INJECT = 4.0
F32 = jnp.float32
BF16 = jnp.bfloat16
HI = lax.Precision.HIGHEST


def split(x):
    hi = x.astype(BF16)
    return hi, (x - hi.astype(F32)).astype(BF16)


def nt(a, b):
    return lax.dot_general(a, b, (((1,), (1,)), ((), ())), preferred_element_type=F32)


def eliminate(lead, rest, off, panels):
    row = lax.broadcasted_iota(jnp.int32, (8, 128), 0)
    count = len(lead)
    wide = len(rest) > 0

    def spread(tile, j):
        return jnp.broadcast_to(tile[j : j + 1], (8, 128))

    def panel(_, carry):
        lead, rest = list(carry[0]), list(carry[1])
        cols = [
            [jnp.broadcast_to(tile[:, off + j : off + j + 1], (8, 128)) for tile in lead]
            for j in range(8)
        ]
        for j in range(0, 8, 2):
            a, b = cols[j], cols[j + 1]
            a0, a1, b0, b1 = spread(a[0], j), spread(a[0], j + 1), spread(b[0], j), spread(b[0], j + 1)
            inv = 1.0 / (a0 * b1 - a1 * b0)
            i00, i01, i10, i11 = b1 * inv, b0 * inv, a1 * inv, a0 * inv

            def sweep(tiles):
                r0, r1 = spread(tiles[0], j), spread(tiles[0], j + 1)
                n0 = i00 * r0 - i01 * r1
                n1 = i11 * r1 - i10 * r0
                out = [tiles[t] - (a[t] * n0 + b[t] * n1) for t in range(count)]
                out[0] = jnp.where(row == j, n0, jnp.where(row == j + 1, n1, out[0]))
                return out

            for later in range(j + 2, 8):
                cols[later] = sweep(cols[later])
            lead = sweep(lead)
            if wide:
                rest = sweep(rest)
        lead = [pltpu.roll(tile, 120, 1) for tile in lead]
        lead = lead[1:] + lead[:1]
        if wide:
            rest = rest[1:] + rest[:1]
        return tuple(lead), tuple(rest)

    return lax.fori_loop(0, panels, panel, (tuple(lead), tuple(rest)))


def tiles_of(x):
    return [x[8 * t : 8 * t + 8] for t in range(x.shape[0] // 8)]


PARTS = 2


def kernel(
    sizes, sig_in, elec_in, order_in, x_in, adj_in, x_out, grad_out,
    fx, fr, fq, fl, fs, cond, sig, elec, order, picked,
    gbufs, r1s, r2s, gfins, gl, gr,
    send, recv, local, s1s, v1s, s2s, v2s, s3s, v3s, s4, v4,
):
    ngx, ngy, nsrc, cx, cy, cols = sizes
    gx, gy, src = lax.axis_index("gx"), lax.axis_index("gy"), lax.axis_index("src")
    half = cols // PARTS

    def peer(axis, index):
        return {"gx": (index, gy, src), "gy": (gx, index, src), "src": (gx, gy, index)}[axis]

    small = [
        pltpu.make_async_copy(sig_in, sig, local.at[0]),
        pltpu.make_async_copy(elec_in, elec, local.at[1]),
        pltpu.make_async_copy(order_in, order, local.at[2]),
    ]
    for copy in small:
        copy.start()

    def load(source, buf, low, count, sem):
        for x in range(cx):
            for y in range(cy):
                pltpu.make_async_copy(
                    source.at[pl.ds(low, count), x, y],
                    buf.at[x + 1, y + 1, pl.ds(low, count)],
                    sem,
                ).start()
        whole = buf.at[pl.ds(1, cx), pl.ds(1, cy), pl.ds(low, count)]
        return pltpu.make_async_copy(whole, whole, sem)

    loads = [load(x_in, fx, h * half, half, local.at[3 + h]) for h in range(PARTS)]

    barrier = pltpu.get_barrier_semaphore()
    groups = (("gx", gx, ngx), ("gy", gy, ngy), ("src", src, nsrc))
    for axis, me, count in groups:
        for k in range(1, count):
            pl.semaphore_signal(
                barrier, inc=1, device_id=peer(axis, lax.rem(me + k, count)), device_id_type=MESH
            )

    def exchange(step, buf, low, count):
        zs = pl.ds(low, count)
        hx, hy = pl.ds(1, cx), pl.ds(1, cy)
        moves = (
            (gx > 0, gx < ngx - 1, buf.at[1, hy, zs], buf.at[cx + 1, hy, zs], ("gx", gx - 1)),
            (gx < ngx - 1, gx > 0, buf.at[cx, hy, zs], buf.at[0, hy, zs], ("gx", gx + 1)),
            (gy > 0, gy < ngy - 1, buf.at[hx, 1, zs], buf.at[hx, cy + 1, zs], ("gy", gy - 1)),
            (gy < ngy - 1, gy > 0, buf.at[hx, cy, zs], buf.at[hx, 0, zs], ("gy", gy + 1)),
        )
        made = []
        for n, (sends, gets, source, target, (axis, index)) in enumerate(moves):
            limit = ngx if axis == "gx" else ngy
            index = jnp.clip(index, 0, limit - 1)
            copy = pltpu.make_async_remote_copy(
                src_ref=source, dst_ref=target, send_sem=send.at[step, n],
                recv_sem=recv.at[step, n], device_id=peer(axis, index), device_id_type=MESH,
            )
            made.append((sends, gets, copy, target))

            @pl.when(sends)
            def _():
                copy.start()

            @pl.when(jnp.logical_not(gets))
            def _():
                target[...] = jnp.zeros(target.shape, F32)

        def arrive():
            for sends, gets, copy, target in made:
                @pl.when(gets)
                def _():
                    copy.wait_recv()

        def leave():
            for sends, gets, copy, target in made:
                @pl.when(sends)
                def _():
                    copy.wait_send()

        leaves.append(leave)
        return arrive

    leaves = []
    for copy in small:
        copy.wait()
    for x in range(cx):
        for y in range(cy):
            fx[x + 1, y + 1, cols:, :] = jnp.broadcast_to(sig[x, y : y + 1, :], (8, 128))
    pl.semaphore_wait(barrier, ngx + ngy + nsrc - 3)
    arrive_sig = exchange(0, fx, cols, 8)
    arrive_x = []
    for h in range(PARTS):
        loads[h].wait()
        arrive_x.append(exchange(1 + h, fx, h * half, half))
    load_l = load(adj_in, fl, 0, cols, local.at[3 + PARTS])

    lane = lax.broadcasted_iota(jnp.int32, (8, 128), 1)

    pairs = elec.shape[1]
    slot = jnp.concatenate([order[...], jnp.full((1, 128 - cols), -1, jnp.int32)], axis=1)
    hit = lax.broadcasted_iota(jnp.int32, (pairs, 128), 0) == jnp.broadcast_to(slot, (pairs, 128))
    table = jnp.concatenate([elec[...].astype(F32), jnp.zeros((6, pairs), F32)], axis=0)
    cells = jnp.dot(table, hit.astype(F32), precision=HI, preferred_element_type=F32).T
    for n in range(2):
        picked[n] = jnp.broadcast_to(cells[:cols, n : n + 1], (cols, 128)).astype(jnp.int32)

    group = 4

    def each_cell(body):
        def step(i, carry):
            x, y = i // (cy // group), group * lax.rem(i, cy // group)
            for k in range(group):
                body(x, y + k)
            return carry

        lax.fori_loop(0, cx * cy // group, step, 0)

    def conductance(x, y):
        def sig_at(i, j):
            return fx[i, j, cols:, :]

        mid = sig_at(x + 1, y + 1)
        parts = [
            0.5 * (mid + sig_at(x, y + 1)),
            0.5 * (mid + sig_at(x + 2, y + 1)),
            0.5 * (mid + sig_at(x + 1, y)),
            0.5 * (mid + sig_at(x + 1, y + 2)),
            0.5 * (mid + jnp.where(lane == 0, 0.0, pltpu.roll(mid, 1, 1))),
            0.5 * (mid + jnp.where(lane == 127, 0.0, pltpu.roll(mid, 127, 1))),
        ]
        total = parts[0] + parts[1] + (parts[2] + parts[3]) + (parts[4] + parts[5])
        parts[4] = jnp.where(lane == 0, 0.0, parts[4])
        parts[5] = jnp.where(lane == 127, 0.0, parts[5])
        for n, part in enumerate(parts + [total]):
            cond[x, y, n] = part

    def image(buf, x, y, h):
        rows = slice(h * half, (h + 1) * half)

        def at(i, j):
            return buf[i, j, rows, :].reshape(half // 8, 8, 128)

        flat = buf[x + 1, y + 1, rows, :]
        mid = flat.reshape(half // 8, 8, 128)
        down = pltpu.roll(flat, 1, 1).reshape(half // 8, 8, 128)
        up = pltpu.roll(flat, 127, 1).reshape(half // 8, 8, 128)
        c = [cond[x, y, n][None] for n in range(7)]
        out = c[6] * mid - (
            c[0] * at(x, y + 1) + c[1] * at(x + 2, y + 1)
            + (c[2] * at(x + 1, y) + c[3] * at(x + 1, y + 2))
            + (c[4] * down + c[5] * up)
        )
        return out.reshape(half, 128)

    arrive_sig()
    each_cell(conductance)

    lane_c = lax.broadcasted_iota(jnp.int32, (half, 128), 1)

    arrive_r = []
    for h in range(PARTS):
        rows = slice(h * half, (h + 1) * half)

        def residual(x, y):
            base = ((gx * cx + x) * (ngy * cy) + gy * cy + y) * 128
            right = jnp.where(picked[0, rows] - base == lane_c, INJECT, 0.0) - jnp.where(
                picked[1, rows] - base == lane_c, INJECT, 0.0
            )
            fr[x + 1, y + 1, rows, :] = right - image(fx, x, y, h)

        arrive_x[h]()
        each_cell(residual)
        arrive_r.append(exchange(1 + PARTS + h, fr, h * half, half))

    arrive_q = []
    for h in range(PARTS):
        def first(x, y):
            fq[x + 1, y + 1, slice(h * half, (h + 1) * half), :] = image(fr, x, y, h)

        arrive_r[h]()
        each_cell(first)
        arrive_q.append(exchange(1 + 2 * PARTS + h, fq, h * half, half))

    def wide_of(buf, o, i):
        x, y = i // (cy // group), group * lax.rem(i, cy // group)
        return split(
            jnp.concatenate([buf[x + o, y + o + k] for k in range(group)], axis=1)
        )

    def times(left, right):
        return nt(left[0], right[0]) + (nt(left[0], right[1]) + nt(left[1], right[0]))

    def early(i, carry):
        r, q = wide_of(fr, 1, i), wide_of(fq, 1, i)
        rq = [jnp.concatenate([u, v], axis=0) for u, v in zip(r, q)]
        return carry[0] + times(r, rq), carry[1] + times(q, q)

    steps = cx * cy // group
    square, double = jnp.zeros((cols, cols), F32), jnp.zeros((cols, 2 * cols), F32)
    g01, g22 = lax.fori_loop(0, steps, early, (double, square))

    late = []

    def reduction(n, value):
        gbuf, r1, r2, gfin = gbufs[n], r1s[n], r2s[n], gfins[n]
        s1, v1, s2, v2, s3, v3 = s1s.at[n], v1s.at[n], s2s.at[n], v2s.at[n], s3s.at[n], v3s.at[n]
        gbuf[...] = value.reshape(gbuf.shape)

        def spread(axis, me, count, pieces, sems, waits):
            made = []
            for k in range(1, count):
                to = lax.rem(me + k, count)
                source, target = pieces(k, to)
                copy = pltpu.make_async_remote_copy(
                    src_ref=source, dst_ref=target, send_sem=sems.at[k - 1],
                    recv_sem=waits.at[k - 1], device_id=peer(axis, to), device_id_type=MESH,
                )
                copy.start()
                made.append(copy)
            late.extend(made)
            return made

        made = spread("gx", gx, ngx, lambda k, to: (gbuf.at[to], r1.at[k - 1]), s1, v1)

        def second():
            share = gbuf[gx]
            for k, copy in enumerate(made):
                copy.wait_recv()
                share = share + r1[k]
            r2[gy] = share
            made[:] = spread("gy", gy, ngy, lambda k, to: (r2.at[gy], r2.at[gy]), s2, v2)

        def third():
            for copy in made:
                copy.wait_recv()
            total = r2[0]
            for k in range(1, ngy):
                total = total + r2[k]
            gfin[gx] = total
            made[:] = spread("gx", gx, ngx, lambda k, to: (gfin.at[gx], gfin.at[gx]), s3, v3)

        def last():
            for copy in made:
                copy.wait_recv()
            return gfin[...].reshape(value.shape)

        return second, third, last

    second_a, third_a, last_a = reduction(
        0, jnp.concatenate([g01, jnp.concatenate([g22, square], axis=1)], axis=0)
    )

    for h in range(PARTS):
        def next_image(x, y):
            fs[x, y, slice(h * half, (h + 1) * half), :] = image(fq, x, y, h)

        arrive_q[h]()
        each_cell(next_image)
    second_a()

    def final(i, carry):
        return carry + times(wide_of(fq, 1, i), wide_of(fs, 0, i))

    g33 = lax.fori_loop(0, steps, final, square)
    second_b, third_b, last_b = reduction(1, jnp.concatenate([g33, square], axis=1))
    third_a()
    second_b()
    whole = last_a()
    top, low = whole[:cols], whole[cols:]
    panels = cols // 8
    state = eliminate(tiles_of(top), tiles_of(low), cols, panels // 2)
    third_b()
    load_l.wait()
    arrive_l = exchange(1 + 3 * PARTS, fl, 0, cols)
    lead, rest = eliminate(*state, cols, panels - panels // 2)
    lead, rest = jnp.concatenate(lead, axis=0), jnp.concatenate(rest, axis=0)
    alpha = lead[:, cols:]
    inv2 = rest[:, :cols]
    g2, g1 = low[:, :cols], top[:, cols:]
    prod = jnp.dot(
        g2, jnp.concatenate([alpha, inv2], axis=1), precision=HI, preferred_element_type=F32
    )
    g3 = last_b()[:, :cols]
    system = jnp.concatenate([g1, g3], axis=1) - prod
    lead, _ = eliminate(tiles_of(system), [], cols, panels)
    c1 = jnp.concatenate(lead, axis=0)[:, cols:]
    c0 = alpha - jnp.dot(inv2, c1, precision=HI, preferred_element_type=F32)
    stacked = jnp.concatenate([c0, c1], axis=0)
    stacked = jnp.concatenate([stacked, jnp.zeros_like(stacked)], axis=1).T[:cols]
    ch, cl = split(stacked)
    factors = jnp.concatenate(
        [
            jnp.concatenate([ch, ch], axis=1),
            jnp.concatenate([cl, jnp.zeros_like(cl)], axis=1),
        ],
        axis=0,
    )

    def advance(x, y):
        def pair(buf):
            return jnp.concatenate([buf[x, y], buf[x, y + 1]], axis=1)

        hi, lo = split(jnp.concatenate([pair(fr), pair(fq)], axis=0))
        out = jnp.dot(factors, jnp.concatenate([hi, lo], axis=0), preferred_element_type=F32)
        out = out[:cols] + out[cols:]
        fx[x, y, :cols, :] = fx[x, y, :cols, :] + out[:, :128]
        fx[x, y + 1, :cols, :] = fx[x, y + 1, :cols, :] + out[:, 128:]

    for leave in leaves:
        leave()
    for x in range(1, cx + 1):
        for y in range(0, cy + 2, 2):
            advance(x, y)
            for row in (y, y + 1):
                if 1 <= row <= cy:
                    pltpu.make_async_copy(
                        fx.at[x, row, pl.ds(0, cols)], x_out.at[:, x - 1, row - 1], local.at[0]
                    ).start()
    for x in (0, cx + 1):
        for y in range(1, cy + 1, 2):
            advance(x, y)

    arrive_l()

    tall = (cols // 8, 8, 128)

    def cell(x, y):
        return fx[x, y, :cols, :], fl[x, y, :, :]

    def rows_of(x):
        return jnp.sum(x.reshape(tall), axis=0)

    def face(x0, y0, x1, y1):
        (u0, l0), (u1, l1) = cell(x0, y0), cell(x1, y1)
        return rows_of((u1 - u0) * (l1 - l0))

    lane_f = lax.broadcasted_iota(jnp.int32, (cols, 128), 1)
    below = [face(0, y, 1, y) for y in range(1, cy + 1)]
    for x in range(1, cx + 1):
        left = face(x, 0, x, 1)
        lines = []
        for y in range(1, cy + 1):
            above, right = face(x, y, x + 1, y), face(x, y, x, y + 1)
            u, l = cell(x, y)
            du = u - jnp.where(lane_f == 0, 0.0, pltpu.roll(u, 1, 1))
            dl = l - jnp.where(lane_f == 0, 0.0, pltpu.roll(l, 1, 1))
            term_z, end = rows_of(du * dl), rows_of(u * l)
            upper = jnp.where(lane == 127, end, pltpu.roll(term_z, 127, 1))
            total = (below[y - 1] + above) + (left + right) + (term_z + upper)
            lines.append(jnp.sum(total, axis=0, keepdims=True))
            below[y - 1], left = above, right
        gl[x - 1] = (-0.5 / cols) * jnp.concatenate(lines, axis=0)

    made = []
    for k in range(1, nsrc):
        copy = pltpu.make_async_remote_copy(
            src_ref=gl, dst_ref=gr.at[k - 1], send_sem=s4.at[k - 1], recv_sem=v4.at[k - 1],
            device_id=peer("src", lax.rem(src + k, nsrc)), device_id_type=MESH,
        )
        copy.start()
        made.append(copy)
    late.extend(made)
    summed = gl[...]
    for k, copy in enumerate(made):
        copy.wait_recv()
        summed = summed + gr[k]
    width = 128 // nsrc
    part = summed[:, :, :width]
    for k in range(1, nsrc):
        part = jnp.where(src == k, summed[:, :, k * width : (k + 1) * width], part)
    grad_out[...] = part
    written = fx.at[pl.ds(1, cx), pl.ds(1, cy), pl.ds(0, cols)]
    pltpu.make_async_copy(written, written, local.at[0]).wait()
    for copy in late:
        copy.wait_send()


def on_device(sizes, conductivity, electrodes, pair_order, initial_fields, adjoint_fields):
    ngx, ngy, nsrc = sizes
    cols, cx, cy, cz = initial_fields.shape
    pairs = electrodes.shape[0]
    dma = pltpu.SemaphoreType.DMA
    full = (cx + 2, cy + 2, cols, cz)
    rows = (2 * cols // ngx, cols // ngx)
    steps = 2 + 3 * PARTS
    return pl.pallas_call(
        functools.partial(kernel, (ngx, ngy, nsrc, cx, cy, cols)),
        out_shape=(
            jax.ShapeDtypeStruct((cols, cx, cy, cz), F32),
            jax.ShapeDtypeStruct((cx, cy, cz // nsrc), F32),
        ),
        in_specs=[pl.BlockSpec(memory_space=pltpu.HBM)] * 5,
        out_specs=(
            pl.BlockSpec(memory_space=pl.ANY),
            pl.BlockSpec(memory_space=pltpu.VMEM),
        ),
        scratch_shapes=[
            pltpu.VMEM((cx + 2, cy + 2, cols + 8, cz), F32),
            pltpu.VMEM(full, F32),
            pltpu.VMEM(full, F32),
            pltpu.VMEM(full, F32),
            pltpu.VMEM((cx, cy, cols, cz), F32),
            pltpu.VMEM((cx, cy, 7, 8, cz), F32),
            pltpu.VMEM((cx, cy, cz), F32),
            pltpu.VMEM((2, pairs), jnp.int32),
            pltpu.VMEM((1, cols), jnp.int32),
            pltpu.VMEM((2, cols, cz), jnp.int32),
            [pltpu.VMEM((ngx, n, 2 * cols), F32) for n in rows],
            [pltpu.VMEM((ngx - 1, n, 2 * cols), F32) for n in rows],
            [pltpu.VMEM((ngy, n, 2 * cols), F32) for n in rows],
            [pltpu.VMEM((ngx, n, 2 * cols), F32) for n in rows],
            pltpu.VMEM((cx, cy, cz), F32),
            pltpu.VMEM((nsrc - 1, cx, cy, cz), F32),
            dma((steps, 4)), dma((steps, 4)), dma((4 + PARTS,)),
            dma((2, ngx - 1)), dma((2, ngx - 1)),
            dma((2, ngy - 1)), dma((2, ngy - 1)),
            dma((2, ngx - 1)), dma((2, ngx - 1)),
            dma((nsrc - 1,)), dma((nsrc - 1,)),
        ],
        compiler_params=pltpu.CompilerParams(
            collective_id=0, has_side_effects=True, vmem_limit_bytes=62 * 1024 * 1024
        ),
        cost_estimate=pl.CostEstimate(
            flops=4 * 10**8, bytes_accessed=2 * 10**6, transcendentals=0
        ),
    )(
        conductivity, electrodes.T, pair_order.reshape(1, cols), initial_fields, adjoint_fields
    )


def solution(mesh):
    sizes = (mesh.shape["gx"], mesh.shape["gy"], mesh.shape["src"])
    field = P("src", "gx", "gy", None)
    return jax.shard_map(
        functools.partial(on_device, sizes),
        mesh=mesh,
        in_specs=(P("gx", "gy", None), P(), P("src"), field, field),
        out_specs=(field, P("gx", "gy", "src")),
        check_vma=False,
    )
```

```python
import functools

import jax
import jax.numpy as jnp
from jax import lax
from jax.experimental import pallas as pl
from jax.experimental.pallas import tpu as pltpu
from jax.sharding import PartitionSpec as P

MESH = pl.DeviceIdType.MESH
INJECT = 4.0
F32 = jnp.float32
BF16 = jnp.bfloat16
HI = lax.Precision.HIGHEST


def split(x):
    hi = x.astype(BF16)
    return hi, (x - hi.astype(F32)).astype(BF16)


def nt(a, b):
    return lax.dot_general(a, b, (((1,), (1,)), ((), ())), preferred_element_type=F32)


def eliminate(lead, rest, off, panels):
    row = lax.broadcasted_iota(jnp.int32, (8, 128), 0)
    count = len(lead)
    wide = len(rest) > 0

    def spread(tile, j):
        return jnp.broadcast_to(tile[j : j + 1], (8, 128))

    def panel(_, carry):
        lead, rest = list(carry[0]), list(carry[1])
        cols = [
            [jnp.broadcast_to(tile[:, off + j : off + j + 1], (8, 128)) for tile in lead]
            for j in range(8)
        ]
        for j in range(0, 8, 2):
            a, b = cols[j], cols[j + 1]
            a0, a1, b0, b1 = spread(a[0], j), spread(a[0], j + 1), spread(b[0], j), spread(b[0], j + 1)
            inv = 1.0 / (a0 * b1 - a1 * b0)
            i00, i01, i10, i11 = b1 * inv, b0 * inv, a1 * inv, a0 * inv

            def sweep(tiles):
                r0, r1 = spread(tiles[0], j), spread(tiles[0], j + 1)
                n0 = i00 * r0 - i01 * r1
                n1 = i11 * r1 - i10 * r0
                out = [tiles[t] - (a[t] * n0 + b[t] * n1) for t in range(count)]
                out[0] = jnp.where(row == j, n0, jnp.where(row == j + 1, n1, out[0]))
                return out

            for later in range(j + 2, 8):
                cols[later] = sweep(cols[later])
            lead = sweep(lead)
            if wide:
                rest = sweep(rest)
        lead = [pltpu.roll(tile, 120, 1) for tile in lead]
        lead = lead[1:] + lead[:1]
        if wide:
            rest = rest[1:] + rest[:1]
        return tuple(lead), tuple(rest)

    return lax.fori_loop(0, panels, panel, (tuple(lead), tuple(rest)))


def tiles_of(x):
    return [x[8 * t : 8 * t + 8] for t in range(x.shape[0] // 8)]


PARTS = 2


def kernel(
    sizes, sig_in, elec_in, order_in, x_in, adj_in, x_out, grad_out,
    fx, fr, fq, fl, fs, cond, sig, elec, order, picked,
    gbufs, r1s, r2s, gfins, gl, gr,
    send, recv, local, s1s, v1s, s2s, v2s, s3s, v3s, s4, v4,
):
    ngx, ngy, nsrc, cx, cy, cols = sizes
    gx, gy, src = lax.axis_index("gx"), lax.axis_index("gy"), lax.axis_index("src")
    half = cols // PARTS

    def peer(axis, index):
        return {"gx": (index, gy, src), "gy": (gx, index, src), "src": (gx, gy, index)}[axis]

    small = [
        pltpu.make_async_copy(sig_in, sig, local.at[0]),
        pltpu.make_async_copy(elec_in, elec, local.at[1]),
        pltpu.make_async_copy(order_in, order, local.at[2]),
    ]
    for copy in small:
        copy.start()

    def load(source, buf, low, count, sem):
        for x in range(cx):
            for y in range(cy):
                pltpu.make_async_copy(
                    source.at[pl.ds(low, count), x, y],
                    buf.at[x + 1, y + 1, pl.ds(low, count)],
                    sem,
                ).start()
        whole = buf.at[pl.ds(1, cx), pl.ds(1, cy), pl.ds(low, count)]
        return pltpu.make_async_copy(whole, whole, sem)

    loads = [load(x_in, fx, h * half, half, local.at[3 + h]) for h in range(PARTS)]

    barrier = pltpu.get_barrier_semaphore()
    groups = (("gx", gx, ngx), ("gy", gy, ngy), ("src", src, nsrc))
    for axis, me, count in groups:
        for k in range(1, count):
            pl.semaphore_signal(
                barrier, inc=1, device_id=peer(axis, lax.rem(me + k, count)), device_id_type=MESH
            )

    def exchange(step, buf, low, count):
        zs = pl.ds(low, count)
        hx, hy = pl.ds(1, cx), pl.ds(1, cy)
        moves = (
            (gx > 0, gx < ngx - 1, buf.at[1, hy, zs], buf.at[cx + 1, hy, zs], ("gx", gx - 1)),
            (gx < ngx - 1, gx > 0, buf.at[cx, hy, zs], buf.at[0, hy, zs], ("gx", gx + 1)),
            (gy > 0, gy < ngy - 1, buf.at[hx, 1, zs], buf.at[hx, cy + 1, zs], ("gy", gy - 1)),
            (gy < ngy - 1, gy > 0, buf.at[hx, cy, zs], buf.at[hx, 0, zs], ("gy", gy + 1)),
        )
        made = []
        for n, (sends, gets, source, target, (axis, index)) in enumerate(moves):
            limit = ngx if axis == "gx" else ngy
            index = jnp.clip(index, 0, limit - 1)
            copy = pltpu.make_async_remote_copy(
                src_ref=source, dst_ref=target, send_sem=send.at[step, n],
                recv_sem=recv.at[step, n], device_id=peer(axis, index), device_id_type=MESH,
            )
            made.append((sends, gets, copy, target))

            @pl.when(sends)
            def _():
                copy.start()

            @pl.when(jnp.logical_not(gets))
            def _():
                target[...] = jnp.zeros(target.shape, F32)

        def arrive():
            for sends, gets, copy, target in made:
                @pl.when(gets)
                def _():
                    copy.wait_recv()

        def leave():
            for sends, gets, copy, target in made:
                @pl.when(sends)
                def _():
                    copy.wait_send()

        leaves.append(leave)
        return arrive

    leaves = []
    for copy in small:
        copy.wait()
    for x in range(cx):
        for y in range(cy):
            fx[x + 1, y + 1, cols:, :] = jnp.broadcast_to(sig[x, y : y + 1, :], (8, 128))
    pl.semaphore_wait(barrier, ngx + ngy + nsrc - 3)
    arrive_sig = exchange(0, fx, cols, 8)
    arrive_x = []
    for h in range(PARTS):
        loads[h].wait()
        arrive_x.append(exchange(1 + h, fx, h * half, half))
    load_l = load(adj_in, fl, 0, cols, local.at[3 + PARTS])

    lane = lax.broadcasted_iota(jnp.int32, (8, 128), 1)

    pairs = elec.shape[1]
    slot = jnp.concatenate([order[...], jnp.full((1, 128 - cols), -1, jnp.int32)], axis=1)
    hit = lax.broadcasted_iota(jnp.int32, (pairs, 128), 0) == jnp.broadcast_to(slot, (pairs, 128))
    table = jnp.concatenate([elec[...].astype(F32), jnp.zeros((6, pairs), F32)], axis=0)
    cells = jnp.dot(table, hit.astype(F32), precision=HI, preferred_element_type=F32).T
    for n in range(2):
        picked[n] = jnp.broadcast_to(cells[:cols, n : n + 1], (cols, 128)).astype(jnp.int32)

    group = 4

    def each_cell(body):
        def step(i, carry):
            x, y = i // (cy // group), group * lax.rem(i, cy // group)
            for k in range(group):
                body(x, y + k)
            return carry

        lax.fori_loop(0, cx * cy // group, step, 0)

    def conductance(x, y):
        def sig_at(i, j):
            return fx[i, j, cols:, :]

        mid = sig_at(x + 1, y + 1)
        parts = [
            0.5 * (mid + sig_at(x, y + 1)),
            0.5 * (mid + sig_at(x + 2, y + 1)),
            0.5 * (mid + sig_at(x + 1, y)),
            0.5 * (mid + sig_at(x + 1, y + 2)),
            0.5 * (mid + jnp.where(lane == 0, 0.0, pltpu.roll(mid, 1, 1))),
            0.5 * (mid + jnp.where(lane == 127, 0.0, pltpu.roll(mid, 127, 1))),
        ]
        total = parts[0] + parts[1] + (parts[2] + parts[3]) + (parts[4] + parts[5])
        parts[4] = jnp.where(lane == 0, 0.0, parts[4])
        parts[5] = jnp.where(lane == 127, 0.0, parts[5])
        for n, part in enumerate(parts + [total]):
            cond[x, y, n] = part

    def image(buf, x, y, h):
        rows = slice(h * half, (h + 1) * half)

        def at(i, j):
            return buf[i, j, rows, :].reshape(half // 8, 8, 128)

        flat = buf[x + 1, y + 1, rows, :]
        mid = flat.reshape(half // 8, 8, 128)
        down = pltpu.roll(flat, 1, 1).reshape(half // 8, 8, 128)
        up = pltpu.roll(flat, 127, 1).reshape(half // 8, 8, 128)
        c = [cond[x, y, n][None] for n in range(7)]
        out = c[6] * mid - (
            c[0] * at(x, y + 1) + c[1] * at(x + 2, y + 1)
            + (c[2] * at(x + 1, y) + c[3] * at(x + 1, y + 2))
            + (c[4] * down + c[5] * up)
        )
        return out.reshape(half, 128)

    arrive_sig()
    each_cell(conductance)

    lane_c = lax.broadcasted_iota(jnp.int32, (half, 128), 1)

    arrive_r = []
    for h in range(PARTS):
        rows = slice(h * half, (h + 1) * half)

        def residual(x, y):
            base = ((gx * cx + x) * (ngy * cy) + gy * cy + y) * 128
            right = jnp.where(picked[0, rows] - base == lane_c, INJECT, 0.0) - jnp.where(
                picked[1, rows] - base == lane_c, INJECT, 0.0
            )
            fr[x + 1, y + 1, rows, :] = right - image(fx, x, y, h)

        arrive_x[h]()
        each_cell(residual)
        arrive_r.append(exchange(1 + PARTS + h, fr, h * half, half))

    arrive_q = []
    for h in range(PARTS):
        def first(x, y):
            fq[x + 1, y + 1, slice(h * half, (h + 1) * half), :] = image(fr, x, y, h)

        arrive_r[h]()
        each_cell(first)
        arrive_q.append(exchange(1 + 2 * PARTS + h, fq, h * half, half))

    def wide_of(buf, o, i):
        x, y = i // (cy // group), group * lax.rem(i, cy // group)
        return split(
            jnp.concatenate([buf[x + o, y + o + k] for k in range(group)], axis=1)
        )

    def times(left, right):
        return nt(left[0], right[0]) + (nt(left[0], right[1]) + nt(left[1], right[0]))

    def early(i, carry):
        r, q = wide_of(fr, 1, i), wide_of(fq, 1, i)
        rq = [jnp.concatenate([u, v], axis=0) for u, v in zip(r, q)]
        return carry[0] + times(r, rq), carry[1] + times(q, q)

    steps = cx * cy // group
    square, double = jnp.zeros((cols, cols), F32), jnp.zeros((cols, 2 * cols), F32)
    g01, g22 = lax.fori_loop(0, steps, early, (double, square))

    late = []

    def reduction(n, value):
        gbuf, r1, r2, gfin = gbufs[n], r1s[n], r2s[n], gfins[n]
        s1, v1, s2, v2, s3, v3 = s1s.at[n], v1s.at[n], s2s.at[n], v2s.at[n], s3s.at[n], v3s.at[n]
        gbuf[...] = value.reshape(gbuf.shape)

        def spread(axis, me, count, pieces, sems, waits):
            made = []
            for k in range(1, count):
                to = lax.rem(me + k, count)
                source, target = pieces(k, to)
                copy = pltpu.make_async_remote_copy(
                    src_ref=source, dst_ref=target, send_sem=sems.at[k - 1],
                    recv_sem=waits.at[k - 1], device_id=peer(axis, to), device_id_type=MESH,
                )
                copy.start()
                made.append(copy)
            late.extend(made)
            return made

        made = spread("gx", gx, ngx, lambda k, to: (gbuf.at[to], r1.at[k - 1]), s1, v1)

        def second():
            share = gbuf[gx]
            for k, copy in enumerate(made):
                copy.wait_recv()
                share = share + r1[k]
            r2[gy] = share
            made[:] = spread("gy", gy, ngy, lambda k, to: (r2.at[gy], r2.at[gy]), s2, v2)

        def third():
            for copy in made:
                copy.wait_recv()
            total = r2[0]
            for k in range(1, ngy):
                total = total + r2[k]
            gfin[gx] = total
            made[:] = spread("gx", gx, ngx, lambda k, to: (gfin.at[gx], gfin.at[gx]), s3, v3)

        def last():
            for copy in made:
                copy.wait_recv()
            return gfin[...].reshape(value.shape)

        return second, third, last

    second_a, third_a, last_a = reduction(
        0, jnp.concatenate([g01, jnp.concatenate([g22, square], axis=1)], axis=0)
    )

    for h in range(PARTS):
        def next_image(x, y):
            fs[x, y, slice(h * half, (h + 1) * half), :] = image(fq, x, y, h)

        arrive_q[h]()
        each_cell(next_image)
        if h == 0:
            second_a()
    third_a()

    def final(i, carry):
        return carry + times(wide_of(fq, 1, i), wide_of(fs, 0, i))

    g33 = lax.fori_loop(0, steps, final, square)
    second_b, third_b, last_b = reduction(1, jnp.concatenate([g33, square], axis=1))
    whole = last_a()
    top, low = whole[:cols], whole[cols:]
    panels = cols // 8
    third = panels // 3
    state = eliminate(tiles_of(top), tiles_of(low), cols, third)
    second_b()
    state = eliminate(*state, cols, third)
    third_b()
    load_l.wait()
    arrive_l = exchange(1 + 3 * PARTS, fl, 0, cols)
    lead, rest = eliminate(*state, cols, panels - 2 * third)
    lead, rest = jnp.concatenate(lead, axis=0), jnp.concatenate(rest, axis=0)
    alpha = lead[:, cols:]
    inv2 = rest[:, :cols]
    g2, g1 = low[:, :cols], top[:, cols:]
    prod = jnp.dot(
        g2, jnp.concatenate([alpha, inv2], axis=1), precision=HI, preferred_element_type=F32
    )
    g3 = last_b()[:, :cols]
    system = jnp.concatenate([g1, g3], axis=1) - prod
    lead, _ = eliminate(tiles_of(system), [], cols, panels)
    c1 = jnp.concatenate(lead, axis=0)[:, cols:]
    c0 = alpha - jnp.dot(inv2, c1, precision=HI, preferred_element_type=F32)
    stacked = jnp.concatenate([c0, c1], axis=0)
    stacked = jnp.concatenate([stacked, jnp.zeros_like(stacked)], axis=1).T[:cols]
    ch, cl = split(stacked)
    factors = jnp.concatenate(
        [
            jnp.concatenate([ch, ch], axis=1),
            jnp.concatenate([cl, jnp.zeros_like(cl)], axis=1),
        ],
        axis=0,
    )

    def advance(x, y):
        def pair(buf):
            return jnp.concatenate([buf[x, y], buf[x, y + 1]], axis=1)

        hi, lo = split(jnp.concatenate([pair(fr), pair(fq)], axis=0))
        out = jnp.dot(factors, jnp.concatenate([hi, lo], axis=0), preferred_element_type=F32)
        out = out[:cols] + out[cols:]
        fx[x, y, :cols, :] = fx[x, y, :cols, :] + out[:, :128]
        fx[x, y + 1, :cols, :] = fx[x, y + 1, :cols, :] + out[:, 128:]

    for leave in leaves:
        leave()
    for x in range(1, cx + 1):
        for y in range(0, cy + 2, 2):
            advance(x, y)
            for row in (y, y + 1):
                if 1 <= row <= cy:
                    pltpu.make_async_copy(
                        fx.at[x, row, pl.ds(0, cols)], x_out.at[:, x - 1, row - 1], local.at[0]
                    ).start()
    for x in (0, cx + 1):
        for y in range(1, cy + 1, 2):
            advance(x, y)

    arrive_l()

    tall = (cols // 8, 8, 128)

    def cell(x, y):
        return fx[x, y, :cols, :], fl[x, y, :, :]

    def rows_of(x):
        return jnp.sum(x.reshape(tall), axis=0)

    def face(x0, y0, x1, y1):
        (u0, l0), (u1, l1) = cell(x0, y0), cell(x1, y1)
        return rows_of((u1 - u0) * (l1 - l0))

    lane_f = lax.broadcasted_iota(jnp.int32, (cols, 128), 1)
    below = [face(0, y, 1, y) for y in range(1, cy + 1)]
    for x in range(1, cx + 1):
        left = face(x, 0, x, 1)
        lines = []
        for y in range(1, cy + 1):
            above, right = face(x, y, x + 1, y), face(x, y, x, y + 1)
            u, l = cell(x, y)
            du = u - jnp.where(lane_f == 0, 0.0, pltpu.roll(u, 1, 1))
            dl = l - jnp.where(lane_f == 0, 0.0, pltpu.roll(l, 1, 1))
            term_z, end = rows_of(du * dl), rows_of(u * l)
            upper = jnp.where(lane == 127, end, pltpu.roll(term_z, 127, 1))
            total = (below[y - 1] + above) + (left + right) + (term_z + upper)
            lines.append(jnp.sum(total, axis=0, keepdims=True))
            below[y - 1], left = above, right
        gl[x - 1] = (-0.5 / cols) * jnp.concatenate(lines, axis=0)

    made = []
    for k in range(1, nsrc):
        copy = pltpu.make_async_remote_copy(
            src_ref=gl, dst_ref=gr.at[k - 1], send_sem=s4.at[k - 1], recv_sem=v4.at[k - 1],
            device_id=peer("src", lax.rem(src + k, nsrc)), device_id_type=MESH,
        )
        copy.start()
        made.append(copy)
    late.extend(made)
    summed = gl[...]
    for k, copy in enumerate(made):
        copy.wait_recv()
        summed = summed + gr[k]
    width = 128 // nsrc
    part = summed[:, :, :width]
    for k in range(1, nsrc):
        part = jnp.where(src == k, summed[:, :, k * width : (k + 1) * width], part)
    grad_out[...] = part
    written = fx.at[pl.ds(1, cx), pl.ds(1, cy), pl.ds(0, cols)]
    pltpu.make_async_copy(written, written, local.at[0]).wait()
    for copy in late:
        copy.wait_send()


def on_device(sizes, conductivity, electrodes, pair_order, initial_fields, adjoint_fields):
    ngx, ngy, nsrc = sizes
    cols, cx, cy, cz = initial_fields.shape
    pairs = electrodes.shape[0]
    dma = pltpu.SemaphoreType.DMA
    full = (cx + 2, cy + 2, cols, cz)
    rows = (2 * cols // ngx, cols // ngx)
    steps = 2 + 3 * PARTS
    return pl.pallas_call(
        functools.partial(kernel, (ngx, ngy, nsrc, cx, cy, cols)),
        out_shape=(
            jax.ShapeDtypeStruct((cols, cx, cy, cz), F32),
            jax.ShapeDtypeStruct((cx, cy, cz // nsrc), F32),
        ),
        in_specs=[pl.BlockSpec(memory_space=pltpu.HBM)] * 5,
        out_specs=(
            pl.BlockSpec(memory_space=pl.ANY),
            pl.BlockSpec(memory_space=pltpu.VMEM),
        ),
        scratch_shapes=[
            pltpu.VMEM((cx + 2, cy + 2, cols + 8, cz), F32),
            pltpu.VMEM(full, F32),
            pltpu.VMEM(full, F32),
            pltpu.VMEM(full, F32),
            pltpu.VMEM((cx, cy, cols, cz), F32),
            pltpu.VMEM((cx, cy, 7, 8, cz), F32),
            pltpu.VMEM((cx, cy, cz), F32),
            pltpu.VMEM((2, pairs), jnp.int32),
            pltpu.VMEM((1, cols), jnp.int32),
            pltpu.VMEM((2, cols, cz), jnp.int32),
            [pltpu.VMEM((ngx, n, 2 * cols), F32) for n in rows],
            [pltpu.VMEM((ngx - 1, n, 2 * cols), F32) for n in rows],
            [pltpu.VMEM((ngy, n, 2 * cols), F32) for n in rows],
            [pltpu.VMEM((ngx, n, 2 * cols), F32) for n in rows],
            pltpu.VMEM((cx, cy, cz), F32),
            pltpu.VMEM((nsrc - 1, cx, cy, cz), F32),
            dma((steps, 4)), dma((steps, 4)), dma((4 + PARTS,)),
            dma((2, ngx - 1)), dma((2, ngx - 1)),
            dma((2, ngy - 1)), dma((2, ngy - 1)),
            dma((2, ngx - 1)), dma((2, ngx - 1)),
            dma((nsrc - 1,)), dma((nsrc - 1,)),
        ],
        compiler_params=pltpu.CompilerParams(
            collective_id=0, has_side_effects=True, vmem_limit_bytes=32 * 1024 * 1024
        ),
        cost_estimate=pl.CostEstimate(
            flops=4 * 10**8, bytes_accessed=2 * 10**6, transcendentals=0
        ),
    )(
        *[
            pltpu.with_memory_space_constraint(value, pltpu.HBM)
            for value in (
                conductivity, electrodes.T, pair_order.reshape(1, cols),
                initial_fields, adjoint_fields,
            )
        ]
    )


def solution(mesh):
    sizes = (mesh.shape["gx"], mesh.shape["gy"], mesh.shape["src"])
    field = P("src", "gx", "gy", None)
    return jax.shard_map(
        functools.partial(on_device, sizes),
        mesh=mesh,
        in_specs=(P("gx", "gy", None), P(), P("src"), field, field),
        out_specs=(field, P("gx", "gy", "src")),
        check_vma=False,
    )
```

```python
import functools

import jax
import jax.numpy as jnp
from jax import lax
from jax.experimental import pallas as pl
from jax.experimental.pallas import tpu as pltpu
from jax.sharding import PartitionSpec as P

MESH = pl.DeviceIdType.MESH
INJECT = 4.0
F32 = jnp.float32
BF16 = jnp.bfloat16
HI = lax.Precision.HIGHEST


def split(x):
    hi = x.astype(BF16)
    return hi, (x - hi.astype(F32)).astype(BF16)


def nt(a, b):
    return lax.dot_general(a, b, (((1,), (1,)), ((), ())), preferred_element_type=F32)


def eliminate(lead, rest, off, panels):
    row = lax.broadcasted_iota(jnp.int32, (8, 128), 0)
    count = len(lead)
    wide = len(rest) > 0

    def spread(tile, j):
        return jnp.broadcast_to(tile[j : j + 1], (8, 128))

    def panel(_, carry):
        lead, rest = list(carry[0]), list(carry[1])
        cols = [
            [jnp.broadcast_to(tile[:, off + j : off + j + 1], (8, 128)) for tile in lead]
            for j in range(8)
        ]
        for j in range(0, 8, 2):
            a, b = cols[j], cols[j + 1]
            a0, a1, b0, b1 = spread(a[0], j), spread(a[0], j + 1), spread(b[0], j), spread(b[0], j + 1)
            inv = 1.0 / (a0 * b1 - a1 * b0)
            i00, i01, i10, i11 = b1 * inv, b0 * inv, a1 * inv, a0 * inv

            def sweep(tiles):
                r0, r1 = spread(tiles[0], j), spread(tiles[0], j + 1)
                n0 = i00 * r0 - i01 * r1
                n1 = i11 * r1 - i10 * r0
                out = [tiles[t] - (a[t] * n0 + b[t] * n1) for t in range(count)]
                out[0] = jnp.where(row == j, n0, jnp.where(row == j + 1, n1, out[0]))
                return out

            for later in range(j + 2, 8):
                cols[later] = sweep(cols[later])
            lead = sweep(lead)
            if wide:
                rest = sweep(rest)
        lead = [pltpu.roll(tile, 120, 1) for tile in lead]
        lead = lead[1:] + lead[:1]
        if wide:
            rest = rest[1:] + rest[:1]
        return tuple(lead), tuple(rest)

    return lax.fori_loop(0, panels, panel, (tuple(lead), tuple(rest)))


def tiles_of(x):
    return [x[8 * t : 8 * t + 8] for t in range(x.shape[0] // 8)]


PARTS = 2


def kernel(
    sizes, sig_in, elec_in, order_in, x_in, adj_in, x_out, grad_out,
    fx, fr, fq, fl, fs, cond, sig, elec, order, picked,
    gbufs, r1s, r2s, gfins, gl, gr,
    send, recv, local, s1s, v1s, s2s, v2s, s3s, v3s, s4, v4,
):
    ngx, ngy, nsrc, cx, cy, cols = sizes
    gx, gy, src = lax.axis_index("gx"), lax.axis_index("gy"), lax.axis_index("src")
    half = cols // PARTS

    def peer(axis, index):
        return {"gx": (index, gy, src), "gy": (gx, index, src), "src": (gx, gy, index)}[axis]

    small = [
        pltpu.make_async_copy(sig_in, sig, local.at[0]),
        pltpu.make_async_copy(elec_in, elec, local.at[1]),
        pltpu.make_async_copy(order_in, order, local.at[2]),
    ]
    for copy in small:
        copy.start()

    def load(source, buf, low, count, sem):
        for x in range(cx):
            for y in range(cy):
                pltpu.make_async_copy(
                    source.at[pl.ds(low, count), x, y],
                    buf.at[x + 1, y + 1, pl.ds(low, count)],
                    sem,
                ).start()
        whole = buf.at[pl.ds(1, cx), pl.ds(1, cy), pl.ds(low, count)]
        return pltpu.make_async_copy(whole, whole, sem)

    loads = [load(x_in, fx, h * half, half, local.at[3 + h]) for h in range(PARTS)]

    barrier = pltpu.get_barrier_semaphore()
    groups = (("gx", gx, ngx), ("gy", gy, ngy), ("src", src, nsrc))
    for axis, me, count in groups:
        for k in range(1, count):
            pl.semaphore_signal(
                barrier, inc=1, device_id=peer(axis, lax.rem(me + k, count)), device_id_type=MESH
            )

    def exchange(step, buf, low, count):
        zs = pl.ds(low, count)
        hx, hy = pl.ds(1, cx), pl.ds(1, cy)
        moves = (
            (gx > 0, gx < ngx - 1, buf.at[1, hy, zs], buf.at[cx + 1, hy, zs], ("gx", gx - 1)),
            (gx < ngx - 1, gx > 0, buf.at[cx, hy, zs], buf.at[0, hy, zs], ("gx", gx + 1)),
            (gy > 0, gy < ngy - 1, buf.at[hx, 1, zs], buf.at[hx, cy + 1, zs], ("gy", gy - 1)),
            (gy < ngy - 1, gy > 0, buf.at[hx, cy, zs], buf.at[hx, 0, zs], ("gy", gy + 1)),
        )
        made = []
        for n, (sends, gets, source, target, (axis, index)) in enumerate(moves):
            limit = ngx if axis == "gx" else ngy
            index = jnp.clip(index, 0, limit - 1)
            copy = pltpu.make_async_remote_copy(
                src_ref=source, dst_ref=target, send_sem=send.at[step, n],
                recv_sem=recv.at[step, n], device_id=peer(axis, index), device_id_type=MESH,
            )
            made.append((sends, gets, copy, target))

            @pl.when(sends)
            def _():
                copy.start()

            @pl.when(jnp.logical_not(gets))
            def _():
                target[...] = jnp.zeros(target.shape, F32)

        def arrive():
            for sends, gets, copy, target in made:
                @pl.when(gets)
                def _():
                    copy.wait_recv()

        def leave():
            for sends, gets, copy, target in made:
                @pl.when(sends)
                def _():
                    copy.wait_send()

        leaves.append(leave)
        return arrive

    leaves = []
    for copy in small:
        copy.wait()
    for x in range(cx):
        for y in range(cy):
            fx[x + 1, y + 1, cols:, :] = jnp.broadcast_to(sig[x, y : y + 1, :], (8, 128))
    pl.semaphore_wait(barrier, ngx + ngy + nsrc - 3)
    arrive_sig = exchange(0, fx, cols, 8)
    arrive_x = []
    for h in range(PARTS):
        loads[h].wait()
        arrive_x.append(exchange(1 + h, fx, h * half, half))
    load_l = load(adj_in, fl, 0, cols, local.at[3 + PARTS])

    lane = lax.broadcasted_iota(jnp.int32, (8, 128), 1)

    pairs = elec.shape[1]
    slot = jnp.concatenate([order[...], jnp.full((1, 128 - cols), -1, jnp.int32)], axis=1)
    hit = lax.broadcasted_iota(jnp.int32, (pairs, 128), 0) == jnp.broadcast_to(slot, (pairs, 128))
    table = jnp.concatenate([elec[...].astype(F32), jnp.zeros((6, pairs), F32)], axis=0)
    cells = jnp.dot(table, hit.astype(F32), precision=HI, preferred_element_type=F32).T
    for n in range(2):
        picked[n] = jnp.broadcast_to(cells[:cols, n : n + 1], (cols, 128)).astype(jnp.int32)

    group = 4

    def each_cell(body):
        def step(i, carry):
            x, y = i // (cy // group), group * lax.rem(i, cy // group)
            for k in range(group):
                body(x, y + k)
            return carry

        lax.fori_loop(0, cx * cy // group, step, 0)

    def conductance(x, y):
        def sig_at(i, j):
            return fx[i, j, cols:, :]

        mid = sig_at(x + 1, y + 1)
        parts = [
            0.5 * (mid + sig_at(x, y + 1)),
            0.5 * (mid + sig_at(x + 2, y + 1)),
            0.5 * (mid + sig_at(x + 1, y)),
            0.5 * (mid + sig_at(x + 1, y + 2)),
            0.5 * (mid + jnp.where(lane == 0, 0.0, pltpu.roll(mid, 1, 1))),
            0.5 * (mid + jnp.where(lane == 127, 0.0, pltpu.roll(mid, 127, 1))),
        ]
        total = parts[0] + parts[1] + (parts[2] + parts[3]) + (parts[4] + parts[5])
        parts[4] = jnp.where(lane == 0, 0.0, parts[4])
        parts[5] = jnp.where(lane == 127, 0.0, parts[5])
        for n, part in enumerate(parts + [total]):
            cond[x, y, n] = part

    def image(buf, x, y, h):
        rows = slice(h * half, (h + 1) * half)

        def at(i, j):
            return buf[i, j, rows, :].reshape(half // 8, 8, 128)

        flat = buf[x + 1, y + 1, rows, :]
        mid = flat.reshape(half // 8, 8, 128)
        down = pltpu.roll(flat, 1, 1).reshape(half // 8, 8, 128)
        up = pltpu.roll(flat, 127, 1).reshape(half // 8, 8, 128)
        c = [cond[x, y, n][None] for n in range(7)]
        out = c[6] * mid - (
            c[0] * at(x, y + 1) + c[1] * at(x + 2, y + 1)
            + (c[2] * at(x + 1, y) + c[3] * at(x + 1, y + 2))
            + (c[4] * down + c[5] * up)
        )
        return out.reshape(half, 128)

    arrive_sig()
    each_cell(conductance)

    lane_c = lax.broadcasted_iota(jnp.int32, (half, 128), 1)

    arrive_r = []
    for h in range(PARTS):
        rows = slice(h * half, (h + 1) * half)

        def residual(x, y):
            base = ((gx * cx + x) * (ngy * cy) + gy * cy + y) * 128
            right = jnp.where(picked[0, rows] - base == lane_c, INJECT, 0.0) - jnp.where(
                picked[1, rows] - base == lane_c, INJECT, 0.0
            )
            fr[x + 1, y + 1, rows, :] = right - image(fx, x, y, h)

        arrive_x[h]()
        each_cell(residual)
        arrive_r.append(exchange(1 + PARTS + h, fr, h * half, half))

    arrive_q = []
    for h in range(PARTS):
        def first(x, y):
            fq[x + 1, y + 1, slice(h * half, (h + 1) * half), :] = image(fr, x, y, h)

        arrive_r[h]()
        each_cell(first)
        arrive_q.append(exchange(1 + 2 * PARTS + h, fq, h * half, half))

    def wide_of(buf, o, i):
        x, y = i // (cy // group), group * lax.rem(i, cy // group)
        return split(
            jnp.concatenate([buf[x + o, y + o + k] for k in range(group)], axis=1)
        )

    def times(left, right):
        return nt(left[0], right[0]) + (nt(left[0], right[1]) + nt(left[1], right[0]))

    def early(i, carry):
        r, q = wide_of(fr, 1, i), wide_of(fq, 1, i)
        rq = [jnp.concatenate([u, v], axis=0) for u, v in zip(r, q)]
        return carry[0] + times(r, rq), carry[1] + times(q, q)

    steps = cx * cy // group
    square, double = jnp.zeros((cols, cols), F32), jnp.zeros((cols, 2 * cols), F32)
    g01, g22 = lax.fori_loop(0, steps, early, (double, square))

    late = []

    def reduction(n, value):
        gbuf, r1, r2, gfin = gbufs[n], r1s[n], r2s[n], gfins[n]
        s1, v1, s2, v2, s3, v3 = s1s.at[n], v1s.at[n], s2s.at[n], v2s.at[n], s3s.at[n], v3s.at[n]
        gbuf[...] = value.reshape(gbuf.shape)

        def spread(axis, me, count, pieces, sems, waits):
            made = []
            for k in range(1, count):
                to = lax.rem(me + k, count)
                source, target = pieces(k, to)
                copy = pltpu.make_async_remote_copy(
                    src_ref=source, dst_ref=target, send_sem=sems.at[k - 1],
                    recv_sem=waits.at[k - 1], device_id=peer(axis, to), device_id_type=MESH,
                )
                copy.start()
                made.append(copy)
            late.extend(made)
            return made

        made = spread("gx", gx, ngx, lambda k, to: (gbuf.at[to], r1.at[k - 1]), s1, v1)

        def second():
            share = gbuf[gx]
            for k, copy in enumerate(made):
                copy.wait_recv()
                share = share + r1[k]
            r2[gy] = share
            made[:] = spread("gy", gy, ngy, lambda k, to: (r2.at[gy], r2.at[gy]), s2, v2)

        def third():
            for copy in made:
                copy.wait_recv()
            total = r2[0]
            for k in range(1, ngy):
                total = total + r2[k]
            gfin[gx] = total
            made[:] = spread("gx", gx, ngx, lambda k, to: (gfin.at[gx], gfin.at[gx]), s3, v3)

        def last():
            for copy in made:
                copy.wait_recv()
            return gfin[...].reshape(value.shape)

        return second, third, last

    second_a, third_a, last_a = reduction(
        0, jnp.concatenate([g01, jnp.concatenate([g22, square], axis=1)], axis=0)
    )

    for h in range(PARTS):
        def next_image(x, y):
            fs[x, y, slice(h * half, (h + 1) * half), :] = image(fq, x, y, h)

        arrive_q[h]()
        each_cell(next_image)
        if h == 0:
            second_a()
    third_a()

    def final(i, carry):
        return carry + times(wide_of(fq, 1, i), wide_of(fs, 0, i))

    g33 = lax.fori_loop(0, steps, final, square)
    second_b, third_b, last_b = reduction(1, jnp.concatenate([g33, square], axis=1))
    whole = last_a()
    top, low = whole[:cols], whole[cols:]
    panels = cols // 8
    third = panels // 3
    state = eliminate(tiles_of(top), tiles_of(low), cols, third)
    second_b()
    state = eliminate(*state, cols, third)
    third_b()
    load_l.wait()
    arrive_l = exchange(1 + 3 * PARTS, fl, 0, cols)
    lead, rest = eliminate(*state, cols, panels - 2 * third)
    lead, rest = jnp.concatenate(lead, axis=0), jnp.concatenate(rest, axis=0)
    alpha = lead[:, cols:]
    inv2 = rest[:, :cols]
    g2, g1 = low[:, :cols], top[:, cols:]
    prod = jnp.dot(
        g2, jnp.concatenate([alpha, inv2], axis=1), precision=HI, preferred_element_type=F32
    )
    g3 = last_b()[:, :cols]
    system = jnp.concatenate([g1, g3], axis=1) - prod
    lead, _ = eliminate(tiles_of(system), [], cols, panels)
    c1 = jnp.concatenate(lead, axis=0)[:, cols:]
    c0 = alpha - jnp.dot(inv2, c1, precision=HI, preferred_element_type=F32)
    stacked = jnp.concatenate([c0, c1], axis=0)
    stacked = jnp.concatenate([stacked, jnp.zeros_like(stacked)], axis=1).T[:cols]
    ch, cl = split(stacked)
    factors = jnp.concatenate(
        [
            jnp.concatenate([ch, ch], axis=1),
            jnp.concatenate([cl, jnp.zeros_like(cl)], axis=1),
        ],
        axis=0,
    )

    def advance(x, y):
        def pair(buf):
            return jnp.concatenate([buf[x, y], buf[x, y + 1]], axis=1)

        hi, lo = split(jnp.concatenate([pair(fr), pair(fq)], axis=0))
        out = jnp.dot(factors, jnp.concatenate([hi, lo], axis=0), preferred_element_type=F32)
        out = out[:cols] + out[cols:]
        for k in range(2):
            new = fx[x, y + k, :cols, :] + out[:, 128 * k : 128 * (k + 1)]
            fx[x, y + k, :cols, :] = new
            if 1 <= x <= cx and 1 <= y + k <= cy:
                x_out[x - 1, y + k - 1] = new

    for leave in leaves:
        leave()
    for x in range(1, cx + 1):
        for y in range(0, cy + 2, 2):
            advance(x, y)
    for x in (0, cx + 1):
        for y in range(1, cy + 1, 2):
            advance(x, y)

    arrive_l()

    tall = (cols // 8, 8, 128)

    def cell(x, y):
        return fx[x, y, :cols, :], fl[x, y, :, :]

    def rows_of(x):
        return jnp.sum(x.reshape(tall), axis=0)

    def face(x0, y0, x1, y1):
        (u0, l0), (u1, l1) = cell(x0, y0), cell(x1, y1)
        return rows_of((u1 - u0) * (l1 - l0))

    lane_f = lax.broadcasted_iota(jnp.int32, (cols, 128), 1)
    below = [face(0, y, 1, y) for y in range(1, cy + 1)]
    for x in range(1, cx + 1):
        left = face(x, 0, x, 1)
        lines = []
        for y in range(1, cy + 1):
            above, right = face(x, y, x + 1, y), face(x, y, x, y + 1)
            u, l = cell(x, y)
            du = u - jnp.where(lane_f == 0, 0.0, pltpu.roll(u, 1, 1))
            dl = l - jnp.where(lane_f == 0, 0.0, pltpu.roll(l, 1, 1))
            term_z, end = rows_of(du * dl), rows_of(u * l)
            upper = jnp.where(lane == 127, end, pltpu.roll(term_z, 127, 1))
            total = (below[y - 1] + above) + (left + right) + (term_z + upper)
            lines.append(jnp.sum(total, axis=0, keepdims=True))
            below[y - 1], left = above, right
        gl[x - 1] = (-0.5 / cols) * jnp.concatenate(lines, axis=0)

    made = []
    for k in range(1, nsrc):
        copy = pltpu.make_async_remote_copy(
            src_ref=gl, dst_ref=gr.at[k - 1], send_sem=s4.at[k - 1], recv_sem=v4.at[k - 1],
            device_id=peer("src", lax.rem(src + k, nsrc)), device_id_type=MESH,
        )
        copy.start()
        made.append(copy)
    late.extend(made)
    summed = gl[...]
    for k, copy in enumerate(made):
        copy.wait_recv()
        summed = summed + gr[k]
    width = 128 // nsrc
    part = summed[:, :, :width]
    for k in range(1, nsrc):
        part = jnp.where(src == k, summed[:, :, k * width : (k + 1) * width], part)
    grad_out[...] = part
    for copy in late:
        copy.wait_send()


def on_device(sizes, conductivity, electrodes, pair_order, initial_fields, adjoint_fields):
    ngx, ngy, nsrc = sizes
    cols, cx, cy, cz = initial_fields.shape
    pairs = electrodes.shape[0]
    dma = pltpu.SemaphoreType.DMA
    full = (cx + 2, cy + 2, cols, cz)
    rows = (2 * cols // ngx, cols // ngx)
    steps = 2 + 3 * PARTS
    x_out, grad = pl.pallas_call(
        functools.partial(kernel, (ngx, ngy, nsrc, cx, cy, cols)),
        out_shape=(
            jax.ShapeDtypeStruct((cx, cy, cols, cz), F32),
            jax.ShapeDtypeStruct((cx, cy, cz // nsrc), F32),
        ),
        in_specs=[pl.BlockSpec(memory_space=pltpu.HBM)] * 5,
        out_specs=(pl.BlockSpec(memory_space=pltpu.VMEM),) * 2,
        scratch_shapes=[
            pltpu.VMEM((cx + 2, cy + 2, cols + 8, cz), F32),
            pltpu.VMEM(full, F32),
            pltpu.VMEM(full, F32),
            pltpu.VMEM(full, F32),
            pltpu.VMEM((cx, cy, cols, cz), F32),
            pltpu.VMEM((cx, cy, 7, 8, cz), F32),
            pltpu.VMEM((cx, cy, cz), F32),
            pltpu.VMEM((2, pairs), jnp.int32),
            pltpu.VMEM((1, cols), jnp.int32),
            pltpu.VMEM((2, cols, cz), jnp.int32),
            [pltpu.VMEM((ngx, n, 2 * cols), F32) for n in rows],
            [pltpu.VMEM((ngx - 1, n, 2 * cols), F32) for n in rows],
            [pltpu.VMEM((ngy, n, 2 * cols), F32) for n in rows],
            [pltpu.VMEM((ngx, n, 2 * cols), F32) for n in rows],
            pltpu.VMEM((cx, cy, cz), F32),
            pltpu.VMEM((nsrc - 1, cx, cy, cz), F32),
            dma((steps, 4)), dma((steps, 4)), dma((4 + PARTS,)),
            dma((2, ngx - 1)), dma((2, ngx - 1)),
            dma((2, ngy - 1)), dma((2, ngy - 1)),
            dma((2, ngx - 1)), dma((2, ngx - 1)),
            dma((nsrc - 1,)), dma((nsrc - 1,)),
        ],
        compiler_params=pltpu.CompilerParams(
            collective_id=0, has_side_effects=True, vmem_limit_bytes=32 * 1024 * 1024
        ),
        cost_estimate=pl.CostEstimate(
            flops=4 * 10**8, bytes_accessed=2 * 10**6, transcendentals=0
        ),
    )(
        *[
            pltpu.with_memory_space_constraint(value, pltpu.HBM)
            for value in (
                conductivity, electrodes.T, pair_order.reshape(1, cols),
                initial_fields, adjoint_fields,
            )
        ]
    )
    return x_out.transpose(2, 0, 1, 3), grad


def solution(mesh):
    sizes = (mesh.shape["gx"], mesh.shape["gy"], mesh.shape["src"])
    field = P("src", "gx", "gy", None)
    return jax.shard_map(
        functools.partial(on_device, sizes),
        mesh=mesh,
        in_specs=(P("gx", "gy", None), P(), P("src"), field, field),
        out_specs=(field, P("gx", "gy", "src")),
        check_vma=False,
    )
```

```python
import functools

import jax
import jax.numpy as jnp
from jax import lax
from jax.experimental import pallas as pl
from jax.experimental.pallas import tpu as pltpu
from jax.sharding import PartitionSpec as P

MESH = pl.DeviceIdType.MESH
INJECT = 4.0
F32 = jnp.float32
BF16 = jnp.bfloat16
HI = lax.Precision.HIGHEST


def split(x):
    hi = x.astype(BF16)
    return hi, (x - hi.astype(F32)).astype(BF16)


def nt(a, b):
    return lax.dot_general(a, b, (((1,), (1,)), ((), ())), preferred_element_type=F32)


def eliminate(lead, rest, off, panels):
    row = lax.broadcasted_iota(jnp.int32, (8, 128), 0)
    count = len(lead)
    wide = len(rest) > 0

    def spread(tile, j):
        return jnp.broadcast_to(tile[j : j + 1], (8, 128))

    def panel(_, carry):
        lead, rest = list(carry[0]), list(carry[1])
        cols = [
            [jnp.broadcast_to(tile[:, off + j : off + j + 1], (8, 128)) for tile in lead]
            for j in range(8)
        ]
        for j in range(0, 8, 2):
            a, b = cols[j], cols[j + 1]
            a0, a1, b0, b1 = spread(a[0], j), spread(a[0], j + 1), spread(b[0], j), spread(b[0], j + 1)
            inv = 1.0 / (a0 * b1 - a1 * b0)
            i00, i01, i10, i11 = b1 * inv, b0 * inv, a1 * inv, a0 * inv

            def sweep(tiles):
                r0, r1 = spread(tiles[0], j), spread(tiles[0], j + 1)
                n0 = i00 * r0 - i01 * r1
                n1 = i11 * r1 - i10 * r0
                out = [tiles[t] - (a[t] * n0 + b[t] * n1) for t in range(count)]
                out[0] = jnp.where(row == j, n0, jnp.where(row == j + 1, n1, out[0]))
                return out

            for later in range(j + 2, 8):
                cols[later] = sweep(cols[later])
            lead = sweep(lead)
            if wide:
                rest = sweep(rest)
        lead = [pltpu.roll(tile, 120, 1) for tile in lead]
        lead = lead[1:] + lead[:1]
        if wide:
            rest = rest[1:] + rest[:1]
        return tuple(lead), tuple(rest)

    return lax.fori_loop(0, panels, panel, (tuple(lead), tuple(rest)))


def tiles_of(x):
    return [x[8 * t : 8 * t + 8] for t in range(x.shape[0] // 8)]


PARTS = 2


def kernel(
    sizes, sig_in, elec_in, order_in, x_in, adj_in, x_out, grad_out,
    fx, fr, fq, fl, fs, cond, sig, elec, order, picked,
    gbufs, r1s, r2s, gfins, gl, gr,
    send, recv, local, s1s, v1s, s2s, v2s, s3s, v3s, s4, v4,
):
    ngx, ngy, nsrc, cx, cy, cols = sizes
    gx, gy, src = lax.axis_index("gx"), lax.axis_index("gy"), lax.axis_index("src")
    half = cols // PARTS

    def peer(axis, index):
        return {"gx": (index, gy, src), "gy": (gx, index, src), "src": (gx, gy, index)}[axis]

    small = [
        pltpu.make_async_copy(sig_in, sig, local.at[0]),
        pltpu.make_async_copy(elec_in, elec, local.at[1]),
        pltpu.make_async_copy(order_in, order, local.at[2]),
    ]
    for copy in small:
        copy.start()

    def load(source, buf, low, count, sem):
        for x in range(cx):
            for y in range(cy):
                pltpu.make_async_copy(
                    source.at[pl.ds(low, count), x, y],
                    buf.at[x + 1, y + 1, pl.ds(low, count)],
                    sem,
                ).start()
        whole = buf.at[pl.ds(1, cx), pl.ds(1, cy), pl.ds(low, count)]
        return pltpu.make_async_copy(whole, whole, sem)

    loads = [load(x_in, fx, h * half, half, local.at[3 + h]) for h in range(PARTS)]

    barrier = pltpu.get_barrier_semaphore()
    groups = (("gx", gx, ngx), ("gy", gy, ngy), ("src", src, nsrc))
    for axis, me, count in groups:
        for k in range(1, count):
            pl.semaphore_signal(
                barrier, inc=1, device_id=peer(axis, lax.rem(me + k, count)), device_id_type=MESH
            )

    def exchange(step, buf, low, count):
        zs = pl.ds(low, count)
        hx, hy = pl.ds(1, cx), pl.ds(1, cy)
        moves = (
            (gx > 0, gx < ngx - 1, buf.at[1, hy, zs], buf.at[cx + 1, hy, zs], ("gx", gx - 1)),
            (gx < ngx - 1, gx > 0, buf.at[cx, hy, zs], buf.at[0, hy, zs], ("gx", gx + 1)),
            (gy > 0, gy < ngy - 1, buf.at[hx, 1, zs], buf.at[hx, cy + 1, zs], ("gy", gy - 1)),
            (gy < ngy - 1, gy > 0, buf.at[hx, cy, zs], buf.at[hx, 0, zs], ("gy", gy + 1)),
        )
        made = []
        for n, (sends, gets, source, target, (axis, index)) in enumerate(moves):
            limit = ngx if axis == "gx" else ngy
            index = jnp.clip(index, 0, limit - 1)
            copy = pltpu.make_async_remote_copy(
                src_ref=source, dst_ref=target, send_sem=send.at[step, n],
                recv_sem=recv.at[step, n], device_id=peer(axis, index), device_id_type=MESH,
            )
            made.append((sends, gets, copy, target))

            @pl.when(sends)
            def _():
                copy.start()

            @pl.when(jnp.logical_not(gets))
            def _():
                target[...] = jnp.zeros(target.shape, F32)

        def arrive():
            for sends, gets, copy, target in made:
                @pl.when(gets)
                def _():
                    copy.wait_recv()

        def leave():
            for sends, gets, copy, target in made:
                @pl.when(sends)
                def _():
                    copy.wait_send()

        leaves.append(leave)
        return arrive

    leaves = []
    for copy in small:
        copy.wait()
    for x in range(cx):
        for y in range(cy):
            fx[x + 1, y + 1, cols:, :] = jnp.broadcast_to(sig[x, y : y + 1, :], (8, 128))
    pl.semaphore_wait(barrier, ngx + ngy + nsrc - 3)
    arrive_sig = exchange(0, fx, cols, 8)
    arrive_x = []
    for h in range(PARTS):
        loads[h].wait()
        arrive_x.append(exchange(1 + h, fx, h * half, half))
    load_l = load(adj_in, fl, 0, cols, local.at[3 + PARTS])

    lane = lax.broadcasted_iota(jnp.int32, (8, 128), 1)

    pairs = elec.shape[1]
    slot = jnp.concatenate([order[...], jnp.full((1, 128 - cols), -1, jnp.int32)], axis=1)
    hit = lax.broadcasted_iota(jnp.int32, (pairs, 128), 0) == jnp.broadcast_to(slot, (pairs, 128))
    table = jnp.concatenate([elec[...].astype(F32), jnp.zeros((6, pairs), F32)], axis=0)
    cells = jnp.dot(table, hit.astype(F32), precision=HI, preferred_element_type=F32).T
    for n in range(2):
        picked[n] = jnp.broadcast_to(cells[:cols, n : n + 1], (cols, 128)).astype(jnp.int32)

    group = 4

    def each_cell(body):
        def step(i, carry):
            x, y = i // (cy // group), group * lax.rem(i, cy // group)
            for k in range(group):
                body(x, y + k)
            return carry

        lax.fori_loop(0, cx * cy // group, step, 0)

    def conductance(x, y):
        def sig_at(i, j):
            return fx[i, j, cols:, :]

        mid = sig_at(x + 1, y + 1)
        parts = [
            0.5 * (mid + sig_at(x, y + 1)),
            0.5 * (mid + sig_at(x + 2, y + 1)),
            0.5 * (mid + sig_at(x + 1, y)),
            0.5 * (mid + sig_at(x + 1, y + 2)),
            0.5 * (mid + jnp.where(lane == 0, 0.0, pltpu.roll(mid, 1, 1))),
            0.5 * (mid + jnp.where(lane == 127, 0.0, pltpu.roll(mid, 127, 1))),
        ]
        total = parts[0] + parts[1] + (parts[2] + parts[3]) + (parts[4] + parts[5])
        parts[4] = jnp.where(lane == 0, 0.0, parts[4])
        parts[5] = jnp.where(lane == 127, 0.0, parts[5])
        for n, part in enumerate(parts + [total]):
            cond[x, y, n] = part

    def image(buf, x, y, h):
        rows = slice(h * half, (h + 1) * half)

        def at(i, j):
            return buf[i, j, rows, :].reshape(half // 8, 8, 128)

        flat = buf[x + 1, y + 1, rows, :]
        mid = flat.reshape(half // 8, 8, 128)
        down = pltpu.roll(flat, 1, 1).reshape(half // 8, 8, 128)
        up = pltpu.roll(flat, 127, 1).reshape(half // 8, 8, 128)
        c = [cond[x, y, n][None] for n in range(7)]
        out = c[6] * mid - (
            c[0] * at(x, y + 1) + c[1] * at(x + 2, y + 1)
            + (c[2] * at(x + 1, y) + c[3] * at(x + 1, y + 2))
            + (c[4] * down + c[5] * up)
        )
        return out.reshape(half, 128)

    arrive_sig()
    each_cell(conductance)

    lane_c = lax.broadcasted_iota(jnp.int32, (half, 128), 1)

    arrive_r = []
    for h in range(PARTS):
        rows = slice(h * half, (h + 1) * half)

        def residual(x, y):
            base = ((gx * cx + x) * (ngy * cy) + gy * cy + y) * 128
            right = jnp.where(picked[0, rows] - base == lane_c, INJECT, 0.0) - jnp.where(
                picked[1, rows] - base == lane_c, INJECT, 0.0
            )
            fr[x + 1, y + 1, rows, :] = right - image(fx, x, y, h)

        arrive_x[h]()
        each_cell(residual)
        arrive_r.append(exchange(1 + PARTS + h, fr, h * half, half))

    arrive_q = []
    for h in range(PARTS):
        def first(x, y):
            fq[x + 1, y + 1, slice(h * half, (h + 1) * half), :] = image(fr, x, y, h)

        arrive_r[h]()
        each_cell(first)
        arrive_q.append(exchange(1 + 2 * PARTS + h, fq, h * half, half))

    def wide_of(buf, o, i):
        x, y = i // (cy // group), group * lax.rem(i, cy // group)
        return split(
            jnp.concatenate([buf[x + o, y + o + k] for k in range(group)], axis=1)
        )

    def times(left, right):
        return nt(left[0], right[0]) + (nt(left[0], right[1]) + nt(left[1], right[0]))

    def early(i, carry):
        r, q = wide_of(fr, 1, i), wide_of(fq, 1, i)
        rq = [jnp.concatenate([u, v], axis=0) for u, v in zip(r, q)]
        return carry[0] + times(r, rq), carry[1] + times(q, q)

    steps = cx * cy // group
    square, double = jnp.zeros((cols, cols), F32), jnp.zeros((cols, 2 * cols), F32)
    g01, g22 = lax.fori_loop(0, steps, early, (double, square))

    late = []

    def reduction(n, value):
        gbuf, r1, r2, gfin = gbufs[n], r1s[n], r2s[n], gfins[n]
        s1, v1, s2, v2, s3, v3 = s1s.at[n], v1s.at[n], s2s.at[n], v2s.at[n], s3s.at[n], v3s.at[n]
        gbuf[...] = value.reshape(gbuf.shape)

        def spread(axis, me, count, pieces, sems, waits):
            made = []
            for k in range(1, count):
                to = lax.rem(me + k, count)
                source, target = pieces(k, to)
                copy = pltpu.make_async_remote_copy(
                    src_ref=source, dst_ref=target, send_sem=sems.at[k - 1],
                    recv_sem=waits.at[k - 1], device_id=peer(axis, to), device_id_type=MESH,
                )
                copy.start()
                made.append(copy)
            late.extend(made)
            return made

        made = spread("gx", gx, ngx, lambda k, to: (gbuf.at[to], r1.at[k - 1]), s1, v1)

        def second():
            share = gbuf[gx]
            for k, copy in enumerate(made):
                copy.wait_recv()
                share = share + r1[k]
            r2[gy] = share
            made[:] = spread("gy", gy, ngy, lambda k, to: (r2.at[gy], r2.at[gy]), s2, v2)

        def third():
            for copy in made:
                copy.wait_recv()
            total = r2[0]
            for k in range(1, ngy):
                total = total + r2[k]
            gfin[gx] = total
            made[:] = spread("gx", gx, ngx, lambda k, to: (gfin.at[gx], gfin.at[gx]), s3, v3)

        def last():
            for copy in made:
                copy.wait_recv()
            return gfin[...].reshape(value.shape)

        return second, third, last

    second_a, third_a, last_a = reduction(
        0, jnp.concatenate([g01, jnp.concatenate([g22, square], axis=1)], axis=0)
    )

    for h in range(PARTS):
        def next_image(x, y):
            fs[x, y, slice(h * half, (h + 1) * half), :] = image(fq, x, y, h)

        arrive_q[h]()
        each_cell(next_image)
    second_a()

    def final(i, carry):
        return carry + times(wide_of(fq, 1, i), wide_of(fs, 0, i))

    g33 = lax.fori_loop(0, steps, final, square)
    second_b, third_b, last_b = reduction(1, jnp.concatenate([g33, square], axis=1))
    third_a()
    second_b()
    whole = last_a()
    top, low = whole[:cols], whole[cols:]
    panels = cols // 8
    state = eliminate(tiles_of(top), tiles_of(low), cols, panels // 2)
    third_b()
    lead, rest = eliminate(*state, cols, panels - panels // 2)
    lead, rest = jnp.concatenate(lead, axis=0), jnp.concatenate(rest, axis=0)
    alpha = lead[:, cols:]
    inv2 = rest[:, :cols]
    g2, g1 = low[:, :cols], top[:, cols:]
    prod = jnp.dot(
        g2, jnp.concatenate([alpha, inv2], axis=1), precision=HI, preferred_element_type=F32
    )
    g3 = last_b()[:, :cols]
    load_l.wait()
    arrive_l = exchange(1 + 3 * PARTS, fl, 0, cols)
    system = jnp.concatenate([g1, g3], axis=1) - prod
    lead, _ = eliminate(tiles_of(system), [], cols, panels)
    c1 = jnp.concatenate(lead, axis=0)[:, cols:]
    c0 = alpha - jnp.dot(inv2, c1, precision=HI, preferred_element_type=F32)
    stacked = jnp.concatenate([c0, c1], axis=0)
    stacked = jnp.concatenate([stacked, jnp.zeros_like(stacked)], axis=1).T[:cols]
    ch, cl = split(stacked)
    factors = jnp.concatenate(
        [
            jnp.concatenate([ch, ch], axis=1),
            jnp.concatenate([cl, jnp.zeros_like(cl)], axis=1),
        ],
        axis=0,
    )

    def advance(x, y):
        def pair(buf):
            return jnp.concatenate([buf[x, y], buf[x, y + 1]], axis=1)

        hi, lo = split(jnp.concatenate([pair(fr), pair(fq)], axis=0))
        out = jnp.dot(factors, jnp.concatenate([hi, lo], axis=0), preferred_element_type=F32)
        out = out[:cols] + out[cols:]
        for k in range(2):
            new = fx[x, y + k, :cols, :] + out[:, 128 * k : 128 * (k + 1)]
            fx[x, y + k, :cols, :] = new
            if 1 <= x <= cx and 1 <= y + k <= cy:
                x_out[x - 1, y + k - 1] = new

    for leave in leaves:
        leave()
    for x in range(1, cx + 1):
        for y in range(0, cy + 2, 2):
            advance(x, y)
    for x in (0, cx + 1):
        for y in range(1, cy + 1, 2):
            advance(x, y)

    arrive_l()

    tall = (cols // 8, 8, 128)

    def cell(x, y):
        return fx[x, y, :cols, :], fl[x, y, :, :]

    def rows_of(x):
        return jnp.sum(x.reshape(tall), axis=0)

    def face(x0, y0, x1, y1):
        (u0, l0), (u1, l1) = cell(x0, y0), cell(x1, y1)
        return rows_of((u1 - u0) * (l1 - l0))

    lane_f = lax.broadcasted_iota(jnp.int32, (cols, 128), 1)
    below = [face(0, y, 1, y) for y in range(1, cy + 1)]
    for x in range(1, cx + 1):
        left = face(x, 0, x, 1)
        lines = []
        for y in range(1, cy + 1):
            above, right = face(x, y, x + 1, y), face(x, y, x, y + 1)
            u, l = cell(x, y)
            du = u - jnp.where(lane_f == 0, 0.0, pltpu.roll(u, 1, 1))
            dl = l - jnp.where(lane_f == 0, 0.0, pltpu.roll(l, 1, 1))
            term_z, end = rows_of(du * dl), rows_of(u * l)
            upper = jnp.where(lane == 127, end, pltpu.roll(term_z, 127, 1))
            total = (below[y - 1] + above) + (left + right) + (term_z + upper)
            lines.append(jnp.sum(total, axis=0, keepdims=True))
            below[y - 1], left = above, right
        gl[x - 1] = (-0.5 / cols) * jnp.concatenate(lines, axis=0)

    made = []
    for k in range(1, nsrc):
        copy = pltpu.make_async_remote_copy(
            src_ref=gl, dst_ref=gr.at[k - 1], send_sem=s4.at[k - 1], recv_sem=v4.at[k - 1],
            device_id=peer("src", lax.rem(src + k, nsrc)), device_id_type=MESH,
        )
        copy.start()
        made.append(copy)
    late.extend(made)
    summed = gl[...]
    for k, copy in enumerate(made):
        copy.wait_recv()
        summed = summed + gr[k]
    width = 128 // nsrc
    part = summed[:, :, :width]
    for k in range(1, nsrc):
        part = jnp.where(src == k, summed[:, :, k * width : (k + 1) * width], part)
    grad_out[...] = part
    for copy in late:
        copy.wait_send()


def on_device(sizes, conductivity, electrodes, pair_order, initial_fields, adjoint_fields):
    ngx, ngy, nsrc = sizes
    cols, cx, cy, cz = initial_fields.shape
    pairs = electrodes.shape[0]
    dma = pltpu.SemaphoreType.DMA
    full = (cx + 2, cy + 2, cols, cz)
    rows = (2 * cols // ngx, cols // ngx)
    steps = 2 + 3 * PARTS
    x_out, grad = pl.pallas_call(
        functools.partial(kernel, (ngx, ngy, nsrc, cx, cy, cols)),
        out_shape=(
            jax.ShapeDtypeStruct((cx, cy, cols, cz), F32),
            jax.ShapeDtypeStruct((cx, cy, cz // nsrc), F32),
        ),
        in_specs=[pl.BlockSpec(memory_space=pltpu.HBM)] * 5,
        out_specs=(pl.BlockSpec(memory_space=pltpu.VMEM),) * 2,
        scratch_shapes=[
            pltpu.VMEM((cx + 2, cy + 2, cols + 8, cz), F32),
            pltpu.VMEM(full, F32),
            pltpu.VMEM(full, F32),
            pltpu.VMEM(full, F32),
            pltpu.VMEM((cx, cy, cols, cz), F32),
            pltpu.VMEM((cx, cy, 7, 8, cz), F32),
            pltpu.VMEM((cx, cy, cz), F32),
            pltpu.VMEM((2, pairs), jnp.int32),
            pltpu.VMEM((1, cols), jnp.int32),
            pltpu.VMEM((2, cols, cz), jnp.int32),
            [pltpu.VMEM((ngx, n, 2 * cols), F32) for n in rows],
            [pltpu.VMEM((ngx - 1, n, 2 * cols), F32) for n in rows],
            [pltpu.VMEM((ngy, n, 2 * cols), F32) for n in rows],
            [pltpu.VMEM((ngx, n, 2 * cols), F32) for n in rows],
            pltpu.VMEM((cx, cy, cz), F32),
            pltpu.VMEM((nsrc - 1, cx, cy, cz), F32),
            dma((steps, 4)), dma((steps, 4)), dma((4 + PARTS,)),
            dma((2, ngx - 1)), dma((2, ngx - 1)),
            dma((2, ngy - 1)), dma((2, ngy - 1)),
            dma((2, ngx - 1)), dma((2, ngx - 1)),
            dma((nsrc - 1,)), dma((nsrc - 1,)),
        ],
        compiler_params=pltpu.CompilerParams(
            collective_id=0, has_side_effects=True, vmem_limit_bytes=32 * 1024 * 1024
        ),
        cost_estimate=pl.CostEstimate(
            flops=4 * 10**8, bytes_accessed=2 * 10**6, transcendentals=0
        ),
    )(
        *[
            pltpu.with_memory_space_constraint(value, pltpu.HBM)
            for value in (
                conductivity, electrodes.T, pair_order.reshape(1, cols),
                initial_fields, adjoint_fields,
            )
        ]
    )
    return x_out.transpose(2, 0, 1, 3), grad


def solution(mesh):
    sizes = (mesh.shape["gx"], mesh.shape["gy"], mesh.shape["src"])
    field = P("src", "gx", "gy", None)
    return jax.shard_map(
        functools.partial(on_device, sizes),
        mesh=mesh,
        in_specs=(P("gx", "gy", None), P(), P("src"), field, field),
        out_specs=(field, P("gx", "gy", "src")),
        check_vma=False,
    )
```

```python
import functools

import jax
import jax.numpy as jnp
from jax import lax
from jax.experimental import pallas as pl
from jax.experimental.pallas import tpu as pltpu
from jax.sharding import PartitionSpec as P

MESH = pl.DeviceIdType.MESH
INJECT = 4.0
F32 = jnp.float32
BF16 = jnp.bfloat16
HI = lax.Precision.HIGHEST


def split(x):
    hi = x.astype(BF16)
    return hi, (x - hi.astype(F32)).astype(BF16)


def nt(a, b):
    return lax.dot_general(a, b, (((1,), (1,)), ((), ())), preferred_element_type=F32)


def eliminate(lead, rest, off, panels):
    row = lax.broadcasted_iota(jnp.int32, (8, 128), 0)
    count = len(lead)
    wide = len(rest) > 0

    def spread(tile, j):
        return jnp.broadcast_to(tile[j : j + 1], (8, 128))

    def panel(_, carry):
        lead, rest = list(carry[0]), list(carry[1])
        cols = [
            [jnp.broadcast_to(tile[:, off + j : off + j + 1], (8, 128)) for tile in lead]
            for j in range(8)
        ]
        for j in range(0, 8, 2):
            a, b = cols[j], cols[j + 1]
            a0, a1, b0, b1 = spread(a[0], j), spread(a[0], j + 1), spread(b[0], j), spread(b[0], j + 1)
            inv = 1.0 / (a0 * b1 - a1 * b0)
            i00, i01, i10, i11 = b1 * inv, b0 * inv, a1 * inv, a0 * inv

            def sweep(tiles):
                r0, r1 = spread(tiles[0], j), spread(tiles[0], j + 1)
                n0 = i00 * r0 - i01 * r1
                n1 = i11 * r1 - i10 * r0
                out = [tiles[t] - (a[t] * n0 + b[t] * n1) for t in range(count)]
                out[0] = jnp.where(row == j, n0, jnp.where(row == j + 1, n1, out[0]))
                return out

            for later in range(j + 2, 8):
                cols[later] = sweep(cols[later])
            lead = sweep(lead)
            if wide:
                rest = sweep(rest)
        lead = [pltpu.roll(tile, 120, 1) for tile in lead]
        lead = lead[1:] + lead[:1]
        if wide:
            rest = rest[1:] + rest[:1]
        return tuple(lead), tuple(rest)

    return lax.fori_loop(0, panels, panel, (tuple(lead), tuple(rest)))


def tiles_of(x):
    return [x[8 * t : 8 * t + 8] for t in range(x.shape[0] // 8)]


PARTS = 2


def kernel(
    sizes, sig_in, elec_in, order_in, x_in, adj_in, x_out, grad_out,
    fx, fr, fq, fl, fs, cond, sig, elec, order, picked,
    gbufs, r1s, r2s, gfins, gl, gr,
    send, recv, local, s1s, v1s, s2s, v2s, s3s, v3s, s4, v4,
):
    ngx, ngy, nsrc, cx, cy, cols = sizes
    gx, gy, src = lax.axis_index("gx"), lax.axis_index("gy"), lax.axis_index("src")
    half = cols // PARTS

    def peer(axis, index):
        return {"gx": (index, gy, src), "gy": (gx, index, src), "src": (gx, gy, index)}[axis]

    small = [
        pltpu.make_async_copy(sig_in, sig, local.at[0]),
        pltpu.make_async_copy(elec_in, elec, local.at[1]),
        pltpu.make_async_copy(order_in, order, local.at[2]),
    ]
    for copy in small:
        copy.start()

    def load(source, buf, low, count, sem):
        for x in range(cx):
            for y in range(cy):
                pltpu.make_async_copy(
                    source.at[pl.ds(low, count), x, y],
                    buf.at[x + 1, y + 1, pl.ds(low, count)],
                    sem,
                ).start()
        whole = buf.at[pl.ds(1, cx), pl.ds(1, cy), pl.ds(low, count)]
        return pltpu.make_async_copy(whole, whole, sem)

    loads = [load(x_in, fx, h * half, half, local.at[3 + h]) for h in range(PARTS)]

    barrier = pltpu.get_barrier_semaphore()
    groups = (("gx", gx, ngx), ("gy", gy, ngy), ("src", src, nsrc))
    for axis, me, count in groups:
        for k in range(1, count):
            pl.semaphore_signal(
                barrier, inc=1, device_id=peer(axis, lax.rem(me + k, count)), device_id_type=MESH
            )

    def exchange(step, buf, low, count):
        zs = pl.ds(low, count)
        hx, hy = pl.ds(1, cx), pl.ds(1, cy)
        moves = (
            (gx > 0, gx < ngx - 1, buf.at[1, hy, zs], buf.at[cx + 1, hy, zs], ("gx", gx - 1)),
            (gx < ngx - 1, gx > 0, buf.at[cx, hy, zs], buf.at[0, hy, zs], ("gx", gx + 1)),
            (gy > 0, gy < ngy - 1, buf.at[hx, 1, zs], buf.at[hx, cy + 1, zs], ("gy", gy - 1)),
            (gy < ngy - 1, gy > 0, buf.at[hx, cy, zs], buf.at[hx, 0, zs], ("gy", gy + 1)),
        )
        made = []
        for n, (sends, gets, source, target, (axis, index)) in enumerate(moves):
            limit = ngx if axis == "gx" else ngy
            index = jnp.clip(index, 0, limit - 1)
            copy = pltpu.make_async_remote_copy(
                src_ref=source, dst_ref=target, send_sem=send.at[step, n],
                recv_sem=recv.at[step, n], device_id=peer(axis, index), device_id_type=MESH,
            )
            made.append((sends, gets, copy, target))

            @pl.when(sends)
            def _():
                copy.start()

            @pl.when(jnp.logical_not(gets))
            def _():
                target[...] = jnp.zeros(target.shape, F32)

        def arrive():
            for sends, gets, copy, target in made:
                @pl.when(gets)
                def _():
                    copy.wait_recv()

        def leave():
            for sends, gets, copy, target in made:
                @pl.when(sends)
                def _():
                    copy.wait_send()

        leaves.append(leave)
        return arrive

    leaves = []
    for copy in small:
        copy.wait()
    for x in range(cx):
        for y in range(cy):
            fx[x + 1, y + 1, cols:, :] = jnp.broadcast_to(sig[x, y : y + 1, :], (8, 128))
    pl.semaphore_wait(barrier, ngx + ngy + nsrc - 3)
    arrive_sig = exchange(0, fx, cols, 8)
    arrive_x = []
    for h in range(PARTS):
        loads[h].wait()
        arrive_x.append(exchange(1 + h, fx, h * half, half))
    load_l = load(adj_in, fl, 0, cols, local.at[3 + PARTS])

    lane = lax.broadcasted_iota(jnp.int32, (8, 128), 1)

    pairs = elec.shape[1]
    slot = jnp.concatenate([order[...], jnp.full((1, 128 - cols), -1, jnp.int32)], axis=1)
    hit = lax.broadcasted_iota(jnp.int32, (pairs, 128), 0) == jnp.broadcast_to(slot, (pairs, 128))
    table = jnp.concatenate([elec[...].astype(F32), jnp.zeros((6, pairs), F32)], axis=0)
    cells = jnp.dot(table, hit.astype(F32), precision=HI, preferred_element_type=F32).T
    for n in range(2):
        picked[n] = jnp.broadcast_to(cells[:cols, n : n + 1], (cols, 128)).astype(jnp.int32)

    group = 4

    def each_cell(body):
        def step(i, carry):
            x, y = i // (cy // group), group * lax.rem(i, cy // group)
            for k in range(group):
                body(x, y + k)
            return carry

        lax.fori_loop(0, cx * cy // group, step, 0)

    def conductance(x, y):
        def sig_at(i, j):
            return fx[i, j, cols:, :]

        mid = sig_at(x + 1, y + 1)
        parts = [
            0.5 * (mid + sig_at(x, y + 1)),
            0.5 * (mid + sig_at(x + 2, y + 1)),
            0.5 * (mid + sig_at(x + 1, y)),
            0.5 * (mid + sig_at(x + 1, y + 2)),
            0.5 * (mid + jnp.where(lane == 0, 0.0, pltpu.roll(mid, 1, 1))),
            0.5 * (mid + jnp.where(lane == 127, 0.0, pltpu.roll(mid, 127, 1))),
        ]
        total = parts[0] + parts[1] + (parts[2] + parts[3]) + (parts[4] + parts[5])
        parts[4] = jnp.where(lane == 0, 0.0, parts[4])
        parts[5] = jnp.where(lane == 127, 0.0, parts[5])
        for n, part in enumerate(parts + [total]):
            cond[x, y, n] = part

    def image(buf, x, y, h):
        rows = slice(h * half, (h + 1) * half)

        def at(i, j):
            return buf[i, j, rows, :].reshape(half // 8, 8, 128)

        flat = buf[x + 1, y + 1, rows, :]
        mid = flat.reshape(half // 8, 8, 128)
        down = pltpu.roll(flat, 1, 1).reshape(half // 8, 8, 128)
        up = pltpu.roll(flat, 127, 1).reshape(half // 8, 8, 128)
        c = [cond[x, y, n][None] for n in range(7)]
        out = c[6] * mid - (
            c[0] * at(x, y + 1) + c[1] * at(x + 2, y + 1)
            + (c[2] * at(x + 1, y) + c[3] * at(x + 1, y + 2))
            + (c[4] * down + c[5] * up)
        )
        return out.reshape(half, 128)

    arrive_sig()
    each_cell(conductance)

    lane_c = lax.broadcasted_iota(jnp.int32, (half, 128), 1)

    arrive_r = []
    for h in range(PARTS):
        rows = slice(h * half, (h + 1) * half)

        def residual(x, y):
            base = ((gx * cx + x) * (ngy * cy) + gy * cy + y) * 128
            right = jnp.where(picked[0, rows] - base == lane_c, INJECT, 0.0) - jnp.where(
                picked[1, rows] - base == lane_c, INJECT, 0.0
            )
            fr[x + 1, y + 1, rows, :] = right - image(fx, x, y, h)

        arrive_x[h]()
        each_cell(residual)
        arrive_r.append(exchange(1 + PARTS + h, fr, h * half, half))

    arrive_q = []
    for h in range(PARTS):
        def first(x, y):
            fq[x + 1, y + 1, slice(h * half, (h + 1) * half), :] = image(fr, x, y, h)

        arrive_r[h]()
        each_cell(first)
        arrive_q.append(exchange(1 + 2 * PARTS + h, fq, h * half, half))

    def wide_of(buf, o, i):
        x, y = i // (cy // group), group * lax.rem(i, cy // group)
        return split(
            jnp.concatenate([buf[x + o, y + o + k] for k in range(group)], axis=1)
        )

    def times(left, right):
        return nt(left[0], right[0]) + (nt(left[0], right[1]) + nt(left[1], right[0]))

    def early(i, carry):
        r, q = wide_of(fr, 1, i), wide_of(fq, 1, i)
        rq = [jnp.concatenate([u, v], axis=0) for u, v in zip(r, q)]
        return carry[0] + times(r, rq), carry[1] + times(q, q)

    steps = cx * cy // group
    square, double = jnp.zeros((cols, cols), F32), jnp.zeros((cols, 2 * cols), F32)
    g01, g22 = lax.fori_loop(0, steps, early, (double, square))

    late = []

    def reduction(n, value):
        gbuf, r1, r2, gfin = gbufs[n], r1s[n], r2s[n], gfins[n]
        s1, v1, s2, v2, s3, v3 = s1s.at[n], v1s.at[n], s2s.at[n], v2s.at[n], s3s.at[n], v3s.at[n]
        gbuf[...] = value.reshape(gbuf.shape)

        def spread(axis, me, count, pieces, sems, waits):
            made = []
            for k in range(1, count):
                to = lax.rem(me + k, count)
                source, target = pieces(k, to)
                copy = pltpu.make_async_remote_copy(
                    src_ref=source, dst_ref=target, send_sem=sems.at[k - 1],
                    recv_sem=waits.at[k - 1], device_id=peer(axis, to), device_id_type=MESH,
                )
                copy.start()
                made.append(copy)
            late.extend(made)
            return made

        made = spread("gx", gx, ngx, lambda k, to: (gbuf.at[to], r1.at[k - 1]), s1, v1)

        def second():
            share = gbuf[gx]
            for k, copy in enumerate(made):
                copy.wait_recv()
                share = share + r1[k]
            r2[gy] = share
            made[:] = spread("gy", gy, ngy, lambda k, to: (r2.at[gy], r2.at[gy]), s2, v2)

        def third():
            for copy in made:
                copy.wait_recv()
            total = r2[0]
            for k in range(1, ngy):
                total = total + r2[k]
            gfin[gx] = total
            made[:] = spread("gx", gx, ngx, lambda k, to: (gfin.at[gx], gfin.at[gx]), s3, v3)

        def last():
            for copy in made:
                copy.wait_recv()
            return gfin[...].reshape(value.shape)

        return second, third, last

    second_a, third_a, last_a = reduction(
        0, jnp.concatenate([g01, jnp.concatenate([g22, square], axis=1)], axis=0)
    )

    for h in range(PARTS):
        def next_image(x, y):
            fs[x, y, slice(h * half, (h + 1) * half), :] = image(fq, x, y, h)

        arrive_q[h]()
        each_cell(next_image)
    second_a()

    def final(i, carry):
        return carry + times(wide_of(fq, 1, i), wide_of(fs, 0, i))

    g33 = lax.fori_loop(0, steps, final, square)
    second_b, third_b, last_b = reduction(1, jnp.concatenate([g33, square], axis=1))
    third_a()
    second_b()
    whole = last_a()
    top, low = whole[:cols], whole[cols:]
    panels = cols // 8
    state = eliminate(tiles_of(top), tiles_of(low), cols, panels // 2)
    third_b()
    load_l.wait()
    arrive_l = exchange(1 + 3 * PARTS, fl, 0, cols)
    lead, rest = eliminate(*state, cols, panels - panels // 2)
    lead, rest = jnp.concatenate(lead, axis=0), jnp.concatenate(rest, axis=0)
    alpha = lead[:, cols:]
    inv2 = rest[:, :cols]
    g2, g1 = low[:, :cols], top[:, cols:]
    prod = jnp.dot(
        g2, jnp.concatenate([alpha, inv2], axis=1), precision=HI, preferred_element_type=F32
    )
    g3 = last_b()[:, :cols]
    system = jnp.concatenate([g1, g3], axis=1) - prod
    lead, _ = eliminate(tiles_of(system), [], cols, panels)
    c1 = jnp.concatenate(lead, axis=0)[:, cols:]
    c0 = alpha - jnp.dot(inv2, c1, precision=HI, preferred_element_type=F32)
    stacked = jnp.concatenate([c0, c1], axis=0)
    stacked = jnp.concatenate([stacked, jnp.zeros_like(stacked)], axis=1).T[:cols]
    ch, cl = split(stacked)
    factors = jnp.concatenate(
        [
            jnp.concatenate([ch, ch], axis=1),
            jnp.concatenate([cl, jnp.zeros_like(cl)], axis=1),
        ],
        axis=0,
    )

    def advance(x, y):
        def pair(buf):
            return jnp.concatenate([buf[x, y], buf[x, y + 1]], axis=1)

        hi, lo = split(jnp.concatenate([pair(fr), pair(fq)], axis=0))
        out = jnp.dot(factors, jnp.concatenate([hi, lo], axis=0), preferred_element_type=F32)
        out = out[:cols] + out[cols:]
        for k in range(2):
            new = fx[x, y + k, :cols, :] + out[:, 128 * k : 128 * (k + 1)]
            fx[x, y + k, :cols, :] = new
            if 1 <= x <= cx and 1 <= y + k <= cy:
                x_out[x - 1, y + k - 1] = new

    for leave in leaves:
        leave()
    for x in range(1, cx + 1):
        for y in range(0, cy + 2, 2):
            advance(x, y)
    for x in (0, cx + 1):
        for y in range(1, cy + 1, 2):
            advance(x, y)

    arrive_l()

    tall = (cols // 8, 8, 128)

    def cell(x, y):
        return fx[x, y, :cols, :], fl[x, y, :, :]

    def rows_of(x):
        return jnp.sum(x.reshape(tall), axis=0)

    def face(x0, y0, x1, y1):
        (u0, l0), (u1, l1) = cell(x0, y0), cell(x1, y1)
        return rows_of((u1 - u0) * (l1 - l0))

    lane_f = lax.broadcasted_iota(jnp.int32, (cols, 128), 1)
    below = [face(0, y, 1, y) for y in range(1, cy + 1)]
    for x in range(1, cx + 1):
        left = face(x, 0, x, 1)
        lines = []
        for y in range(1, cy + 1):
            above, right = face(x, y, x + 1, y), face(x, y, x, y + 1)
            u, l = cell(x, y)
            du = u - jnp.where(lane_f == 0, 0.0, pltpu.roll(u, 1, 1))
            dl = l - jnp.where(lane_f == 0, 0.0, pltpu.roll(l, 1, 1))
            term_z, end = rows_of(du * dl), rows_of(u * l)
            upper = jnp.where(lane == 127, end, pltpu.roll(term_z, 127, 1))
            total = (below[y - 1] + above) + (left + right) + (term_z + upper)
            lines.append(jnp.sum(total, axis=0, keepdims=True))
            below[y - 1], left = above, right
        gl[x - 1] = (-0.5 / cols) * jnp.concatenate(lines, axis=0)

    made = []
    for k in range(1, nsrc):
        copy = pltpu.make_async_remote_copy(
            src_ref=gl, dst_ref=gr.at[k - 1], send_sem=s4.at[k - 1], recv_sem=v4.at[k - 1],
            device_id=peer("src", lax.rem(src + k, nsrc)), device_id_type=MESH,
        )
        copy.start()
        made.append(copy)
    late.extend(made)
    summed = gl[...]
    for k, copy in enumerate(made):
        copy.wait_recv()
        summed = summed + gr[k]
    width = 128 // nsrc
    part = summed[:, :, :width]
    for k in range(1, nsrc):
        part = jnp.where(src == k, summed[:, :, k * width : (k + 1) * width], part)
    grad_out[...] = part
    for copy in late:
        copy.wait_send()


def on_device(sizes, conductivity, electrodes, pair_order, initial_fields, adjoint_fields):
    ngx, ngy, nsrc = sizes
    cols, cx, cy, cz = initial_fields.shape
    pairs = electrodes.shape[0]
    dma = pltpu.SemaphoreType.DMA
    full = (cx + 2, cy + 2, cols, cz)
    rows = (2 * cols // ngx, cols // ngx)
    steps = 2 + 3 * PARTS
    x_out, grad = pl.pallas_call(
        functools.partial(kernel, (ngx, ngy, nsrc, cx, cy, cols)),
        out_shape=(
            jax.ShapeDtypeStruct((cx, cy, cols, cz), F32),
            jax.ShapeDtypeStruct((cx, cy, cz // nsrc), F32),
        ),
        in_specs=[pl.BlockSpec(memory_space=pltpu.HBM)] * 5,
        out_specs=(pl.BlockSpec(memory_space=pltpu.VMEM),) * 2,
        scratch_shapes=[
            pltpu.VMEM((cx + 2, cy + 2, cols + 8, cz), F32),
            pltpu.VMEM(full, F32),
            pltpu.VMEM(full, F32),
            pltpu.VMEM(full, F32),
            pltpu.VMEM((cx, cy, cols, cz), F32),
            pltpu.VMEM((cx, cy, 7, 8, cz), F32),
            pltpu.VMEM((cx, cy, cz), F32),
            pltpu.VMEM((2, pairs), jnp.int32),
            pltpu.VMEM((1, cols), jnp.int32),
            pltpu.VMEM((2, cols, cz), jnp.int32),
            [pltpu.VMEM((ngx, n, 2 * cols), F32) for n in rows],
            [pltpu.VMEM((ngx - 1, n, 2 * cols), F32) for n in rows],
            [pltpu.VMEM((ngy, n, 2 * cols), F32) for n in rows],
            [pltpu.VMEM((ngx, n, 2 * cols), F32) for n in rows],
            pltpu.VMEM((cx, cy, cz), F32),
            pltpu.VMEM((nsrc - 1, cx, cy, cz), F32),
            dma((steps, 4)), dma((steps, 4)), dma((4 + PARTS,)),
            dma((2, ngx - 1)), dma((2, ngx - 1)),
            dma((2, ngy - 1)), dma((2, ngy - 1)),
            dma((2, ngx - 1)), dma((2, ngx - 1)),
            dma((nsrc - 1,)), dma((nsrc - 1,)),
        ],
        compiler_params=pltpu.CompilerParams(
            collective_id=0, has_side_effects=True, vmem_limit_bytes=32 * 1024 * 1024
        ),
        cost_estimate=pl.CostEstimate(
            flops=4 * 10**8, bytes_accessed=2 * 10**6, transcendentals=0
        ),
    )(
        *[
            pltpu.with_memory_space_constraint(value, pltpu.HBM)
            for value in (
                conductivity, electrodes.T, pair_order.reshape(1, cols),
                initial_fields, adjoint_fields,
            )
        ]
    )
    return x_out.transpose(2, 0, 1, 3), grad


def solution(mesh):
    sizes = (mesh.shape["gx"], mesh.shape["gy"], mesh.shape["src"])
    field = P("src", "gx", "gy", None)
    return jax.shard_map(
        functools.partial(on_device, sizes),
        mesh=mesh,
        in_specs=(P("gx", "gy", None), P(), P("src"), field, field),
        out_specs=(field, P("gx", "gy", "src")),
        check_vma=False,
    )
```

```python
import functools

import jax
import jax.numpy as jnp
from jax import lax
from jax.experimental import pallas as pl
from jax.experimental.pallas import tpu as pltpu
from jax.sharding import PartitionSpec as P

MESH = pl.DeviceIdType.MESH
INJECT = 4.0
F32 = jnp.float32
BF16 = jnp.bfloat16
HI = lax.Precision.HIGHEST


def split(x):
    hi = x.astype(BF16)
    return hi, (x - hi.astype(F32)).astype(BF16)


def nt(a, b):
    return lax.dot_general(a, b, (((1,), (1,)), ((), ())), preferred_element_type=F32)


def eliminate(lead, rest, off, panels):
    row = lax.broadcasted_iota(jnp.int32, (8, 128), 0)
    count = len(lead)
    wide = len(rest) > 0

    def spread(tile, j):
        return jnp.broadcast_to(tile[j : j + 1], (8, 128))

    def panel(_, carry):
        lead, rest = list(carry[0]), list(carry[1])
        cols = [
            [jnp.broadcast_to(tile[:, off + j : off + j + 1], (8, 128)) for tile in lead]
            for j in range(8)
        ]
        for j in range(0, 8, 2):
            a, b = cols[j], cols[j + 1]
            a0, a1, b0, b1 = spread(a[0], j), spread(a[0], j + 1), spread(b[0], j), spread(b[0], j + 1)
            inv = 1.0 / (a0 * b1 - a1 * b0)
            i00, i01, i10, i11 = b1 * inv, b0 * inv, a1 * inv, a0 * inv

            def sweep(tiles):
                r0, r1 = spread(tiles[0], j), spread(tiles[0], j + 1)
                n0 = i00 * r0 - i01 * r1
                n1 = i11 * r1 - i10 * r0
                out = [tiles[t] - (a[t] * n0 + b[t] * n1) for t in range(count)]
                out[0] = jnp.where(row == j, n0, jnp.where(row == j + 1, n1, out[0]))
                return out

            for later in range(j + 2, 8):
                cols[later] = sweep(cols[later])
            lead = sweep(lead)
            if wide:
                rest = sweep(rest)
        lead = [pltpu.roll(tile, 120, 1) for tile in lead]
        lead = lead[1:] + lead[:1]
        if wide:
            rest = rest[1:] + rest[:1]
        return tuple(lead), tuple(rest)

    return lax.fori_loop(0, panels, panel, (tuple(lead), tuple(rest)))


def tiles_of(x):
    return [x[8 * t : 8 * t + 8] for t in range(x.shape[0] // 8)]


PARTS = 4


def kernel(
    sizes, sig_in, elec_in, order_in, x_in, adj_in, x_out, grad_out,
    fx, fr, fq, fl, fs, cond, sig, elec, order, picked,
    gbufs, r1s, r2s, gfins, gl, gr,
    send, recv, local, s1s, v1s, s2s, v2s, s3s, v3s, s4, v4,
):
    ngx, ngy, nsrc, cx, cy, cols = sizes
    gx, gy, src = lax.axis_index("gx"), lax.axis_index("gy"), lax.axis_index("src")
    half = cols // PARTS

    def peer(axis, index):
        return {"gx": (index, gy, src), "gy": (gx, index, src), "src": (gx, gy, index)}[axis]

    small = [
        pltpu.make_async_copy(sig_in, sig, local.at[0]),
        pltpu.make_async_copy(elec_in, elec, local.at[1]),
        pltpu.make_async_copy(order_in, order, local.at[2]),
    ]
    for copy in small:
        copy.start()

    def load(source, buf, low, count, sem):
        for x in range(cx):
            for y in range(cy):
                pltpu.make_async_copy(
                    source.at[pl.ds(low, count), x, y],
                    buf.at[x + 1, y + 1, pl.ds(low, count)],
                    sem,
                ).start()
        whole = buf.at[pl.ds(1, cx), pl.ds(1, cy), pl.ds(low, count)]
        return pltpu.make_async_copy(whole, whole, sem)

    loads = [load(x_in, fx, h * half, half, local.at[3 + h]) for h in range(PARTS)]

    barrier = pltpu.get_barrier_semaphore()
    groups = (("gx", gx, ngx), ("gy", gy, ngy), ("src", src, nsrc))
    for axis, me, count in groups:
        for k in range(1, count):
            pl.semaphore_signal(
                barrier, inc=1, device_id=peer(axis, lax.rem(me + k, count)), device_id_type=MESH
            )

    def exchange(step, buf, low, count):
        zs = pl.ds(low, count)
        hx, hy = pl.ds(1, cx), pl.ds(1, cy)
        moves = (
            (gx > 0, gx < ngx - 1, buf.at[1, hy, zs], buf.at[cx + 1, hy, zs], ("gx", gx - 1)),
            (gx < ngx - 1, gx > 0, buf.at[cx, hy, zs], buf.at[0, hy, zs], ("gx", gx + 1)),
            (gy > 0, gy < ngy - 1, buf.at[hx, 1, zs], buf.at[hx, cy + 1, zs], ("gy", gy - 1)),
            (gy < ngy - 1, gy > 0, buf.at[hx, cy, zs], buf.at[hx, 0, zs], ("gy", gy + 1)),
        )
        made = []
        for n, (sends, gets, source, target, (axis, index)) in enumerate(moves):
            limit = ngx if axis == "gx" else ngy
            index = jnp.clip(index, 0, limit - 1)
            copy = pltpu.make_async_remote_copy(
                src_ref=source, dst_ref=target, send_sem=send.at[step, n],
                recv_sem=recv.at[step, n], device_id=peer(axis, index), device_id_type=MESH,
            )
            made.append((sends, gets, copy, target))

            @pl.when(sends)
            def _():
                copy.start()

            @pl.when(jnp.logical_not(gets))
            def _():
                target[...] = jnp.zeros(target.shape, F32)

        def arrive():
            for sends, gets, copy, target in made:
                @pl.when(gets)
                def _():
                    copy.wait_recv()

        def leave():
            for sends, gets, copy, target in made:
                @pl.when(sends)
                def _():
                    copy.wait_send()

        leaves.append(leave)
        return arrive

    leaves = []
    for copy in small:
        copy.wait()
    for x in range(cx):
        for y in range(cy):
            fx[x + 1, y + 1, cols:, :] = jnp.broadcast_to(sig[x, y : y + 1, :], (8, 128))
    pl.semaphore_wait(barrier, ngx + ngy + nsrc - 3)
    arrive_sig = exchange(0, fx, cols, 8)
    arrive_x = []
    for h in range(PARTS):
        loads[h].wait()
        arrive_x.append(exchange(1 + h, fx, h * half, half))
    load_l = load(adj_in, fl, 0, cols, local.at[3 + PARTS])

    lane = lax.broadcasted_iota(jnp.int32, (8, 128), 1)

    pairs = elec.shape[1]
    slot = jnp.concatenate([order[...], jnp.full((1, 128 - cols), -1, jnp.int32)], axis=1)
    hit = lax.broadcasted_iota(jnp.int32, (pairs, 128), 0) == jnp.broadcast_to(slot, (pairs, 128))
    table = jnp.concatenate([elec[...].astype(F32), jnp.zeros((6, pairs), F32)], axis=0)
    cells = jnp.dot(table, hit.astype(F32), precision=HI, preferred_element_type=F32).T
    for n in range(2):
        picked[n] = jnp.broadcast_to(cells[:cols, n : n + 1], (cols, 128)).astype(jnp.int32)

    group = 4

    bunch = cy

    def each_cell(body):
        def step(i, carry):
            x, y = i // (cy // bunch), bunch * lax.rem(i, cy // bunch)
            for k in range(bunch):
                body(x, y + k)
            return carry

        lax.fori_loop(0, cx * cy // bunch, step, 0)

    def conductance(x, y):
        def sig_at(i, j):
            return fx[i, j, cols:, :]

        mid = sig_at(x + 1, y + 1)
        parts = [
            0.5 * (mid + sig_at(x, y + 1)),
            0.5 * (mid + sig_at(x + 2, y + 1)),
            0.5 * (mid + sig_at(x + 1, y)),
            0.5 * (mid + sig_at(x + 1, y + 2)),
            0.5 * (mid + jnp.where(lane == 0, 0.0, pltpu.roll(mid, 1, 1))),
            0.5 * (mid + jnp.where(lane == 127, 0.0, pltpu.roll(mid, 127, 1))),
        ]
        total = parts[0] + parts[1] + (parts[2] + parts[3]) + (parts[4] + parts[5])
        parts[4] = jnp.where(lane == 0, 0.0, parts[4])
        parts[5] = jnp.where(lane == 127, 0.0, parts[5])
        for n, part in enumerate(parts + [total]):
            cond[x, y, n] = part

    def image(buf, x, y, h):
        rows = slice(h * half, (h + 1) * half)

        def at(i, j):
            return buf[i, j, rows, :].reshape(half // 8, 8, 128)

        flat = buf[x + 1, y + 1, rows, :]
        mid = flat.reshape(half // 8, 8, 128)
        down = pltpu.roll(flat, 1, 1).reshape(half // 8, 8, 128)
        up = pltpu.roll(flat, 127, 1).reshape(half // 8, 8, 128)
        c = [cond[x, y, n][None] for n in range(7)]
        out = c[6] * mid - (
            c[0] * at(x, y + 1) + c[1] * at(x + 2, y + 1)
            + (c[2] * at(x + 1, y) + c[3] * at(x + 1, y + 2))
            + (c[4] * down + c[5] * up)
        )
        return out.reshape(half, 128)

    arrive_sig()
    each_cell(conductance)

    lane_c = lax.broadcasted_iota(jnp.int32, (half, 128), 1)

    arrive_r = []
    for h in range(PARTS):
        rows = slice(h * half, (h + 1) * half)

        def residual(x, y):
            base = ((gx * cx + x) * (ngy * cy) + gy * cy + y) * 128
            right = jnp.where(picked[0, rows] - base == lane_c, INJECT, 0.0) - jnp.where(
                picked[1, rows] - base == lane_c, INJECT, 0.0
            )
            fr[x + 1, y + 1, rows, :] = right - image(fx, x, y, h)

        arrive_x[h]()
        each_cell(residual)
        arrive_r.append(exchange(1 + PARTS + h, fr, h * half, half))

    arrive_q = []
    for h in range(PARTS):
        def first(x, y):
            fq[x + 1, y + 1, slice(h * half, (h + 1) * half), :] = image(fr, x, y, h)

        arrive_r[h]()
        each_cell(first)
        arrive_q.append(exchange(1 + 2 * PARTS + h, fq, h * half, half))

    def wide_of(buf, o, i):
        x, y = i // (cy // group), group * lax.rem(i, cy // group)
        return split(
            jnp.concatenate([buf[x + o, y + o + k] for k in range(group)], axis=1)
        )

    def times(left, right):
        return nt(left[0], right[0]) + (nt(left[0], right[1]) + nt(left[1], right[0]))

    def early(i, carry):
        r, q = wide_of(fr, 1, i), wide_of(fq, 1, i)
        rq = [jnp.concatenate([u, v], axis=0) for u, v in zip(r, q)]
        return carry[0] + times(r, rq), carry[1] + times(q, q)

    steps = cx * cy // group
    square, double = jnp.zeros((cols, cols), F32), jnp.zeros((cols, 2 * cols), F32)
    g01, g22 = lax.fori_loop(0, steps, early, (double, square))

    late = []

    def reduction(n, value):
        gbuf, r1, r2, gfin = gbufs[n], r1s[n], r2s[n], gfins[n]
        s1, v1, s2, v2, s3, v3 = s1s.at[n], v1s.at[n], s2s.at[n], v2s.at[n], s3s.at[n], v3s.at[n]
        gbuf[...] = value.reshape(gbuf.shape)

        def spread(axis, me, count, pieces, sems, waits):
            made = []
            for k in range(1, count):
                to = lax.rem(me + k, count)
                source, target = pieces(k, to)
                copy = pltpu.make_async_remote_copy(
                    src_ref=source, dst_ref=target, send_sem=sems.at[k - 1],
                    recv_sem=waits.at[k - 1], device_id=peer(axis, to), device_id_type=MESH,
                )
                copy.start()
                made.append(copy)
            late.extend(made)
            return made

        made = spread("gx", gx, ngx, lambda k, to: (gbuf.at[to], r1.at[k - 1]), s1, v1)

        def second():
            share = gbuf[gx]
            for k, copy in enumerate(made):
                copy.wait_recv()
                share = share + r1[k]
            r2[gy] = share
            made[:] = spread("gy", gy, ngy, lambda k, to: (r2.at[gy], r2.at[gy]), s2, v2)

        def third():
            for copy in made:
                copy.wait_recv()
            total = r2[0]
            for k in range(1, ngy):
                total = total + r2[k]
            gfin[gx] = total
            made[:] = spread("gx", gx, ngx, lambda k, to: (gfin.at[gx], gfin.at[gx]), s3, v3)

        def last():
            for copy in made:
                copy.wait_recv()
            return gfin[...].reshape(value.shape)

        return second, third, last

    second_a, third_a, last_a = reduction(
        0, jnp.concatenate([g01, jnp.concatenate([g22, square], axis=1)], axis=0)
    )

    for h in range(PARTS):
        def next_image(x, y):
            fs[x, y, slice(h * half, (h + 1) * half), :] = image(fq, x, y, h)

        arrive_q[h]()
        each_cell(next_image)
    second_a()

    def final(i, carry):
        return carry + times(wide_of(fq, 1, i), wide_of(fs, 0, i))

    g33 = lax.fori_loop(0, steps, final, square)
    second_b, third_b, last_b = reduction(1, jnp.concatenate([g33, square], axis=1))
    third_a()
    second_b()
    whole = last_a()
    top, low = whole[:cols], whole[cols:]
    panels = cols // 8
    state = eliminate(tiles_of(top), tiles_of(low), cols, panels // 2)
    third_b()
    load_l.wait()
    arrive_l = exchange(1 + 3 * PARTS, fl, 0, cols)
    lead, rest = eliminate(*state, cols, panels - panels // 2)
    lead, rest = jnp.concatenate(lead, axis=0), jnp.concatenate(rest, axis=0)
    alpha = lead[:, cols:]
    inv2 = rest[:, :cols]
    g2, g1 = low[:, :cols], top[:, cols:]
    prod = jnp.dot(
        g2, jnp.concatenate([alpha, inv2], axis=1), precision=HI, preferred_element_type=F32
    )
    g3 = last_b()[:, :cols]
    system = jnp.concatenate([g1, g3], axis=1) - prod
    lead, _ = eliminate(tiles_of(system), [], cols, panels)
    c1 = jnp.concatenate(lead, axis=0)[:, cols:]
    c0 = alpha - jnp.dot(inv2, c1, precision=HI, preferred_element_type=F32)
    stacked = jnp.concatenate([c0, c1], axis=0)
    stacked = jnp.concatenate([stacked, jnp.zeros_like(stacked)], axis=1).T[:cols]
    ch, cl = split(stacked)
    factors = jnp.concatenate(
        [
            jnp.concatenate([ch, ch], axis=1),
            jnp.concatenate([cl, jnp.zeros_like(cl)], axis=1),
        ],
        axis=0,
    )

    def advance(x, y):
        def pair(buf):
            return jnp.concatenate([buf[x, y], buf[x, y + 1]], axis=1)

        hi, lo = split(jnp.concatenate([pair(fr), pair(fq)], axis=0))
        out = jnp.dot(factors, jnp.concatenate([hi, lo], axis=0), preferred_element_type=F32)
        out = out[:cols] + out[cols:]
        for k in range(2):
            new = fx[x, y + k, :cols, :] + out[:, 128 * k : 128 * (k + 1)]
            fx[x, y + k, :cols, :] = new
            if 1 <= x <= cx and 1 <= y + k <= cy:
                x_out[x - 1, y + k - 1] = new

    for leave in leaves:
        leave()
    for x in range(1, cx + 1):
        for y in range(0, cy + 2, 2):
            advance(x, y)
    for x in (0, cx + 1):
        for y in range(1, cy + 1, 2):
            advance(x, y)

    arrive_l()

    tall = (cols // 8, 8, 128)

    def cell(x, y):
        return fx[x, y, :cols, :], fl[x, y, :, :]

    def rows_of(x):
        return jnp.sum(x.reshape(tall), axis=0)

    def face(x0, y0, x1, y1):
        (u0, l0), (u1, l1) = cell(x0, y0), cell(x1, y1)
        return rows_of((u1 - u0) * (l1 - l0))

    lane_f = lax.broadcasted_iota(jnp.int32, (cols, 128), 1)
    below = [face(0, y, 1, y) for y in range(1, cy + 1)]
    for x in range(1, cx + 1):
        left = face(x, 0, x, 1)
        lines = []
        for y in range(1, cy + 1):
            above, right = face(x, y, x + 1, y), face(x, y, x, y + 1)
            u, l = cell(x, y)
            du = u - jnp.where(lane_f == 0, 0.0, pltpu.roll(u, 1, 1))
            dl = l - jnp.where(lane_f == 0, 0.0, pltpu.roll(l, 1, 1))
            term_z, end = rows_of(du * dl), rows_of(u * l)
            upper = jnp.where(lane == 127, end, pltpu.roll(term_z, 127, 1))
            total = (below[y - 1] + above) + (left + right) + (term_z + upper)
            lines.append(jnp.sum(total, axis=0, keepdims=True))
            below[y - 1], left = above, right
        gl[x - 1] = (-0.5 / cols) * jnp.concatenate(lines, axis=0)

    made = []
    for k in range(1, nsrc):
        copy = pltpu.make_async_remote_copy(
            src_ref=gl, dst_ref=gr.at[k - 1], send_sem=s4.at[k - 1], recv_sem=v4.at[k - 1],
            device_id=peer("src", lax.rem(src + k, nsrc)), device_id_type=MESH,
        )
        copy.start()
        made.append(copy)
    late.extend(made)
    summed = gl[...]
    for k, copy in enumerate(made):
        copy.wait_recv()
        summed = summed + gr[k]
    width = 128 // nsrc
    part = summed[:, :, :width]
    for k in range(1, nsrc):
        part = jnp.where(src == k, summed[:, :, k * width : (k + 1) * width], part)
    grad_out[...] = part
    for copy in late:
        copy.wait_send()


def on_device(sizes, conductivity, electrodes, pair_order, initial_fields, adjoint_fields):
    ngx, ngy, nsrc = sizes
    cols, cx, cy, cz = initial_fields.shape
    pairs = electrodes.shape[0]
    dma = pltpu.SemaphoreType.DMA
    full = (cx + 2, cy + 2, cols, cz)
    rows = (2 * cols // ngx, cols // ngx)
    steps = 2 + 3 * PARTS
    x_out, grad = pl.pallas_call(
        functools.partial(kernel, (ngx, ngy, nsrc, cx, cy, cols)),
        out_shape=(
            jax.ShapeDtypeStruct((cx, cy, cols, cz), F32),
            jax.ShapeDtypeStruct((cx, cy, cz // nsrc), F32),
        ),
        in_specs=[pl.BlockSpec(memory_space=pltpu.HBM)] * 5,
        out_specs=(pl.BlockSpec(memory_space=pltpu.VMEM),) * 2,
        scratch_shapes=[
            pltpu.VMEM((cx + 2, cy + 2, cols + 8, cz), F32),
            pltpu.VMEM(full, F32),
            pltpu.VMEM(full, F32),
            pltpu.VMEM(full, F32),
            pltpu.VMEM((cx, cy, cols, cz), F32),
            pltpu.VMEM((cx, cy, 7, 8, cz), F32),
            pltpu.VMEM((cx, cy, cz), F32),
            pltpu.VMEM((2, pairs), jnp.int32),
            pltpu.VMEM((1, cols), jnp.int32),
            pltpu.VMEM((2, cols, cz), jnp.int32),
            [pltpu.VMEM((ngx, n, 2 * cols), F32) for n in rows],
            [pltpu.VMEM((ngx - 1, n, 2 * cols), F32) for n in rows],
            [pltpu.VMEM((ngy, n, 2 * cols), F32) for n in rows],
            [pltpu.VMEM((ngx, n, 2 * cols), F32) for n in rows],
            pltpu.VMEM((cx, cy, cz), F32),
            pltpu.VMEM((nsrc - 1, cx, cy, cz), F32),
            dma((steps, 4)), dma((steps, 4)), dma((4 + PARTS,)),
            dma((2, ngx - 1)), dma((2, ngx - 1)),
            dma((2, ngy - 1)), dma((2, ngy - 1)),
            dma((2, ngx - 1)), dma((2, ngx - 1)),
            dma((nsrc - 1,)), dma((nsrc - 1,)),
        ],
        compiler_params=pltpu.CompilerParams(
            collective_id=0, has_side_effects=True, vmem_limit_bytes=32 * 1024 * 1024
        ),
        cost_estimate=pl.CostEstimate(
            flops=4 * 10**8, bytes_accessed=2 * 10**6, transcendentals=0
        ),
    )(
        *[
            pltpu.with_memory_space_constraint(value, pltpu.HBM)
            for value in (
                conductivity, electrodes.T, pair_order.reshape(1, cols),
                initial_fields, adjoint_fields,
            )
        ]
    )
    return x_out.transpose(2, 0, 1, 3), grad


def solution(mesh):
    sizes = (mesh.shape["gx"], mesh.shape["gy"], mesh.shape["src"])
    field = P("src", "gx", "gy", None)
    return jax.shard_map(
        functools.partial(on_device, sizes),
        mesh=mesh,
        in_specs=(P("gx", "gy", None), P(), P("src"), field, field),
        out_specs=(field, P("gx", "gy", "src")),
        check_vma=False,
    )
```

```python
import functools

import jax
import jax.numpy as jnp
from jax import lax
from jax.experimental import pallas as pl
from jax.experimental.pallas import tpu as pltpu
from jax.sharding import PartitionSpec as P

MESH = pl.DeviceIdType.MESH
INJECT = 4.0
F32 = jnp.float32
BF16 = jnp.bfloat16
HI = lax.Precision.HIGHEST


def split(x):
    hi = x.astype(BF16)
    return hi, (x - hi.astype(F32)).astype(BF16)


def nt(a, b):
    return lax.dot_general(a, b, (((1,), (1,)), ((), ())), preferred_element_type=F32)


def eliminate(lead, rest, off, panels):
    row = lax.broadcasted_iota(jnp.int32, (8, 128), 0)
    count = len(lead)
    wide = len(rest) > 0

    def spread(tile, j):
        return jnp.broadcast_to(tile[j : j + 1], (8, 128))

    def panel(_, carry):
        lead, rest = list(carry[0]), list(carry[1])
        cols = [
            [jnp.broadcast_to(tile[:, off + j : off + j + 1], (8, 128)) for tile in lead]
            for j in range(8)
        ]
        for j in range(0, 8, 2):
            a, b = cols[j], cols[j + 1]
            a0, a1, b0, b1 = spread(a[0], j), spread(a[0], j + 1), spread(b[0], j), spread(b[0], j + 1)
            inv = 1.0 / (a0 * b1 - a1 * b0)
            i00, i01, i10, i11 = b1 * inv, b0 * inv, a1 * inv, a0 * inv

            def sweep(tiles):
                r0, r1 = spread(tiles[0], j), spread(tiles[0], j + 1)
                n0 = i00 * r0 - i01 * r1
                n1 = i11 * r1 - i10 * r0
                out = [tiles[t] - (a[t] * n0 + b[t] * n1) for t in range(count)]
                out[0] = jnp.where(row == j, n0, jnp.where(row == j + 1, n1, out[0]))
                return out

            for later in range(j + 2, 8):
                cols[later] = sweep(cols[later])
            lead = sweep(lead)
            if wide:
                rest = sweep(rest)
        lead = [pltpu.roll(tile, 120, 1) for tile in lead]
        lead = lead[1:] + lead[:1]
        if wide:
            rest = rest[1:] + rest[:1]
        return tuple(lead), tuple(rest)

    def pair(step, carry):
        return panel(step, panel(step, carry))

    return lax.fori_loop(0, panels // 2, pair, (tuple(lead), tuple(rest)))


def tiles_of(x):
    return [x[8 * t : 8 * t + 8] for t in range(x.shape[0] // 8)]


PARTS = 4


def kernel(
    sizes, sig_in, elec_in, order_in, x_in, adj_in, x_out, grad_out,
    fx, fr, fq, fl, fs, cond, sig, elec, order, picked,
    gbufs, r1s, r2s, gfins, gl, gr,
    send, recv, local, s1s, v1s, s2s, v2s, s3s, v3s, s4, v4,
):
    ngx, ngy, nsrc, cx, cy, cols = sizes
    gx, gy, src = lax.axis_index("gx"), lax.axis_index("gy"), lax.axis_index("src")
    half = cols // PARTS

    def peer(axis, index):
        return {"gx": (index, gy, src), "gy": (gx, index, src), "src": (gx, gy, index)}[axis]

    small = [
        pltpu.make_async_copy(sig_in, sig, local.at[0]),
        pltpu.make_async_copy(elec_in, elec, local.at[1]),
        pltpu.make_async_copy(order_in, order, local.at[2]),
    ]
    for copy in small:
        copy.start()

    def load(source, buf, low, count, sem):
        for x in range(cx):
            for y in range(cy):
                pltpu.make_async_copy(
                    source.at[pl.ds(low, count), x, y],
                    buf.at[x + 1, y + 1, pl.ds(low, count)],
                    sem,
                ).start()
        whole = buf.at[pl.ds(1, cx), pl.ds(1, cy), pl.ds(low, count)]
        return pltpu.make_async_copy(whole, whole, sem)

    loads = [load(x_in, fx, h * half, half, local.at[3 + h]) for h in range(PARTS)]

    barrier = pltpu.get_barrier_semaphore()
    groups = (("gx", gx, ngx), ("gy", gy, ngy), ("src", src, nsrc))
    for axis, me, count in groups:
        for k in range(1, count):
            pl.semaphore_signal(
                barrier, inc=1, device_id=peer(axis, lax.rem(me + k, count)), device_id_type=MESH
            )

    def exchange(step, buf, low, count):
        zs = pl.ds(low, count)
        hx, hy = pl.ds(1, cx), pl.ds(1, cy)
        moves = (
            (gx > 0, gx < ngx - 1, buf.at[1, hy, zs], buf.at[cx + 1, hy, zs], ("gx", gx - 1)),
            (gx < ngx - 1, gx > 0, buf.at[cx, hy, zs], buf.at[0, hy, zs], ("gx", gx + 1)),
            (gy > 0, gy < ngy - 1, buf.at[hx, 1, zs], buf.at[hx, cy + 1, zs], ("gy", gy - 1)),
            (gy < ngy - 1, gy > 0, buf.at[hx, cy, zs], buf.at[hx, 0, zs], ("gy", gy + 1)),
        )
        made = []
        for n, (sends, gets, source, target, (axis, index)) in enumerate(moves):
            limit = ngx if axis == "gx" else ngy
            index = jnp.clip(index, 0, limit - 1)
            copy = pltpu.make_async_remote_copy(
                src_ref=source, dst_ref=target, send_sem=send.at[step, n],
                recv_sem=recv.at[step, n], device_id=peer(axis, index), device_id_type=MESH,
            )
            made.append((sends, gets, copy, target))

            @pl.when(sends)
            def _():
                copy.start()

            @pl.when(jnp.logical_not(gets))
            def _():
                target[...] = jnp.zeros(target.shape, F32)

        def arrive():
            for sends, gets, copy, target in made:
                @pl.when(gets)
                def _():
                    copy.wait_recv()

        def leave():
            for sends, gets, copy, target in made:
                @pl.when(sends)
                def _():
                    copy.wait_send()

        leaves.append(leave)
        return arrive

    leaves = []
    for copy in small:
        copy.wait()
    for x in range(cx):
        for y in range(cy):
            fx[x + 1, y + 1, cols:, :] = jnp.broadcast_to(sig[x, y : y + 1, :], (8, 128))
    pl.semaphore_wait(barrier, ngx + ngy + nsrc - 3)
    arrive_sig = exchange(0, fx, cols, 8)
    arrive_x = []
    for h in range(PARTS):
        loads[h].wait()
        arrive_x.append(exchange(1 + h, fx, h * half, half))
    load_l = load(adj_in, fl, 0, cols, local.at[3 + PARTS])

    lane = lax.broadcasted_iota(jnp.int32, (8, 128), 1)

    pairs = elec.shape[1]
    slot = jnp.concatenate([order[...], jnp.full((1, 128 - cols), -1, jnp.int32)], axis=1)
    hit = lax.broadcasted_iota(jnp.int32, (pairs, 128), 0) == jnp.broadcast_to(slot, (pairs, 128))
    table = jnp.concatenate([elec[...].astype(F32), jnp.zeros((6, pairs), F32)], axis=0)
    cells = jnp.dot(table, hit.astype(F32), precision=HI, preferred_element_type=F32).T
    for n in range(2):
        picked[n] = jnp.broadcast_to(cells[:cols, n : n + 1], (cols, 128)).astype(jnp.int32)

    group = 4

    bunch = cy

    def each_cell(body):
        def step(i, carry):
            x, y = i // (cy // bunch), bunch * lax.rem(i, cy // bunch)
            for k in range(bunch):
                body(x, y + k)
            return carry

        lax.fori_loop(0, cx * cy // bunch, step, 0)

    def conductance(x, y):
        def sig_at(i, j):
            return fx[i, j, cols:, :]

        mid = sig_at(x + 1, y + 1)
        parts = [
            0.5 * (mid + sig_at(x, y + 1)),
            0.5 * (mid + sig_at(x + 2, y + 1)),
            0.5 * (mid + sig_at(x + 1, y)),
            0.5 * (mid + sig_at(x + 1, y + 2)),
            0.5 * (mid + jnp.where(lane == 0, 0.0, pltpu.roll(mid, 1, 1))),
            0.5 * (mid + jnp.where(lane == 127, 0.0, pltpu.roll(mid, 127, 1))),
        ]
        total = parts[0] + parts[1] + (parts[2] + parts[3]) + (parts[4] + parts[5])
        parts[4] = jnp.where(lane == 0, 0.0, parts[4])
        parts[5] = jnp.where(lane == 127, 0.0, parts[5])
        for n, part in enumerate(parts + [total]):
            cond[x, y, n] = part

    def image(buf, x, y, h):
        rows = slice(h * half, (h + 1) * half)

        def at(i, j):
            return buf[i, j, rows, :].reshape(half // 8, 8, 128)

        flat = buf[x + 1, y + 1, rows, :]
        mid = flat.reshape(half // 8, 8, 128)
        down = pltpu.roll(flat, 1, 1).reshape(half // 8, 8, 128)
        up = pltpu.roll(flat, 127, 1).reshape(half // 8, 8, 128)
        c = [cond[x, y, n][None] for n in range(7)]
        out = c[6] * mid - (
            c[0] * at(x, y + 1) + c[1] * at(x + 2, y + 1)
            + (c[2] * at(x + 1, y) + c[3] * at(x + 1, y + 2))
            + (c[4] * down + c[5] * up)
        )
        return out.reshape(half, 128)

    arrive_sig()
    each_cell(conductance)

    lane_c = lax.broadcasted_iota(jnp.int32, (half, 128), 1)

    arrive_r = []
    for h in range(PARTS):
        rows = slice(h * half, (h + 1) * half)

        def residual(x, y):
            base = ((gx * cx + x) * (ngy * cy) + gy * cy + y) * 128
            right = jnp.where(picked[0, rows] - base == lane_c, INJECT, 0.0) - jnp.where(
                picked[1, rows] - base == lane_c, INJECT, 0.0
            )
            fr[x + 1, y + 1, rows, :] = right - image(fx, x, y, h)

        arrive_x[h]()
        each_cell(residual)
        arrive_r.append(exchange(1 + PARTS + h, fr, h * half, half))

    arrive_q = []
    for h in range(PARTS):
        def first(x, y):
            fq[x + 1, y + 1, slice(h * half, (h + 1) * half), :] = image(fr, x, y, h)

        arrive_r[h]()
        each_cell(first)
        arrive_q.append(exchange(1 + 2 * PARTS + h, fq, h * half, half))

    def wide_of(buf, o, i):
        x, y = i // (cy // group), group * lax.rem(i, cy // group)
        return split(
            jnp.concatenate([buf[x + o, y + o + k] for k in range(group)], axis=1)
        )

    def times(left, right):
        return nt(left[0], right[0]) + (nt(left[0], right[1]) + nt(left[1], right[0]))

    def early(i, carry):
        r, q = wide_of(fr, 1, i), wide_of(fq, 1, i)
        rq = [jnp.concatenate([u, v], axis=0) for u, v in zip(r, q)]
        return carry[0] + times(r, rq), carry[1] + times(q, q)

    steps = cx * cy // group
    square, double = jnp.zeros((cols, cols), F32), jnp.zeros((cols, 2 * cols), F32)
    g01, g22 = lax.fori_loop(0, steps, early, (double, square))

    late = []

    def reduction(n, value):
        gbuf, r1, r2, gfin = gbufs[n], r1s[n], r2s[n], gfins[n]
        s1, v1, s2, v2, s3, v3 = s1s.at[n], v1s.at[n], s2s.at[n], v2s.at[n], s3s.at[n], v3s.at[n]
        gbuf[...] = value.reshape(gbuf.shape)

        def spread(axis, me, count, pieces, sems, waits):
            made = []
            for k in range(1, count):
                to = lax.rem(me + k, count)
                source, target = pieces(k, to)
                copy = pltpu.make_async_remote_copy(
                    src_ref=source, dst_ref=target, send_sem=sems.at[k - 1],
                    recv_sem=waits.at[k - 1], device_id=peer(axis, to), device_id_type=MESH,
                )
                copy.start()
                made.append(copy)
            late.extend(made)
            return made

        made = spread("gx", gx, ngx, lambda k, to: (gbuf.at[to], r1.at[k - 1]), s1, v1)

        def second():
            share = gbuf[gx]
            for k, copy in enumerate(made):
                copy.wait_recv()
                share = share + r1[k]
            r2[gy] = share
            made[:] = spread("gy", gy, ngy, lambda k, to: (r2.at[gy], r2.at[gy]), s2, v2)

        def third():
            for copy in made:
                copy.wait_recv()
            total = r2[0]
            for k in range(1, ngy):
                total = total + r2[k]
            gfin[gx] = total
            made[:] = spread("gx", gx, ngx, lambda k, to: (gfin.at[gx], gfin.at[gx]), s3, v3)

        def last():
            for copy in made:
                copy.wait_recv()
            return gfin[...].reshape(value.shape)

        return second, third, last

    second_a, third_a, last_a = reduction(
        0, jnp.concatenate([g01, jnp.concatenate([g22, square], axis=1)], axis=0)
    )

    for h in range(PARTS):
        def next_image(x, y):
            fs[x, y, slice(h * half, (h + 1) * half), :] = image(fq, x, y, h)

        arrive_q[h]()
        each_cell(next_image)
    second_a()

    def final(i, carry):
        return carry + times(wide_of(fq, 1, i), wide_of(fs, 0, i))

    g33 = lax.fori_loop(0, steps, final, square)
    second_b, third_b, last_b = reduction(1, jnp.concatenate([g33, square], axis=1))
    third_a()
    second_b()
    whole = last_a()
    top, low = whole[:cols], whole[cols:]
    panels = cols // 8
    state = eliminate(tiles_of(top), tiles_of(low), cols, panels // 2)
    third_b()
    load_l.wait()
    arrive_l = exchange(1 + 3 * PARTS, fl, 0, cols)
    lead, rest = eliminate(*state, cols, panels - panels // 2)
    lead, rest = jnp.concatenate(lead, axis=0), jnp.concatenate(rest, axis=0)
    alpha = lead[:, cols:]
    inv2 = rest[:, :cols]
    g2, g1 = low[:, :cols], top[:, cols:]
    prod = jnp.dot(
        g2, jnp.concatenate([alpha, inv2], axis=1), precision=HI, preferred_element_type=F32
    )
    g3 = last_b()[:, :cols]
    system = jnp.concatenate([g1, g3], axis=1) - prod
    lead, _ = eliminate(tiles_of(system), [], cols, panels)
    c1 = jnp.concatenate(lead, axis=0)[:, cols:]
    c0 = alpha - jnp.dot(inv2, c1, precision=HI, preferred_element_type=F32)
    stacked = jnp.concatenate([c0, c1], axis=0)
    stacked = jnp.concatenate([stacked, jnp.zeros_like(stacked)], axis=1).T[:cols]
    ch, cl = split(stacked)
    factors = jnp.concatenate(
        [
            jnp.concatenate([ch, ch], axis=1),
            jnp.concatenate([cl, jnp.zeros_like(cl)], axis=1),
        ],
        axis=0,
    )

    def advance(x, y):
        def pair(buf):
            return jnp.concatenate([buf[x, y], buf[x, y + 1]], axis=1)

        hi, lo = split(jnp.concatenate([pair(fr), pair(fq)], axis=0))
        out = jnp.dot(factors, jnp.concatenate([hi, lo], axis=0), preferred_element_type=F32)
        out = out[:cols] + out[cols:]
        for k in range(2):
            new = fx[x, y + k, :cols, :] + out[:, 128 * k : 128 * (k + 1)]
            fx[x, y + k, :cols, :] = new
            if 1 <= x <= cx and 1 <= y + k <= cy:
                x_out[x - 1, y + k - 1] = new

    for leave in leaves:
        leave()
    for x in range(1, cx + 1):
        for y in range(0, cy + 2, 2):
            advance(x, y)
    for x in (0, cx + 1):
        for y in range(1, cy + 1, 2):
            advance(x, y)

    arrive_l()

    tall = (cols // 8, 8, 128)

    def cell(x, y):
        return fx[x, y, :cols, :], fl[x, y, :, :]

    def rows_of(x):
        return jnp.sum(x.reshape(tall), axis=0)

    def face(x0, y0, x1, y1):
        (u0, l0), (u1, l1) = cell(x0, y0), cell(x1, y1)
        return rows_of((u1 - u0) * (l1 - l0))

    lane_f = lax.broadcasted_iota(jnp.int32, (cols, 128), 1)
    below = [face(0, y, 1, y) for y in range(1, cy + 1)]
    for x in range(1, cx + 1):
        left = face(x, 0, x, 1)
        lines = []
        for y in range(1, cy + 1):
            above, right = face(x, y, x + 1, y), face(x, y, x, y + 1)
            u, l = cell(x, y)
            du = u - jnp.where(lane_f == 0, 0.0, pltpu.roll(u, 1, 1))
            dl = l - jnp.where(lane_f == 0, 0.0, pltpu.roll(l, 1, 1))
            term_z, end = rows_of(du * dl), rows_of(u * l)
            upper = jnp.where(lane == 127, end, pltpu.roll(term_z, 127, 1))
            total = (below[y - 1] + above) + (left + right) + (term_z + upper)
            lines.append(jnp.sum(total, axis=0, keepdims=True))
            below[y - 1], left = above, right
        gl[x - 1] = (-0.5 / cols) * jnp.concatenate(lines, axis=0)

    made = []
    for k in range(1, nsrc):
        copy = pltpu.make_async_remote_copy(
            src_ref=gl, dst_ref=gr.at[k - 1], send_sem=s4.at[k - 1], recv_sem=v4.at[k - 1],
            device_id=peer("src", lax.rem(src + k, nsrc)), device_id_type=MESH,
        )
        copy.start()
        made.append(copy)
    late.extend(made)
    summed = gl[...]
    for k, copy in enumerate(made):
        copy.wait_recv()
        summed = summed + gr[k]
    width = 128 // nsrc
    part = summed[:, :, :width]
    for k in range(1, nsrc):
        part = jnp.where(src == k, summed[:, :, k * width : (k + 1) * width], part)
    grad_out[...] = part
    for copy in late:
        copy.wait_send()


def on_device(sizes, conductivity, electrodes, pair_order, initial_fields, adjoint_fields):
    ngx, ngy, nsrc = sizes
    cols, cx, cy, cz = initial_fields.shape
    pairs = electrodes.shape[0]
    dma = pltpu.SemaphoreType.DMA
    full = (cx + 2, cy + 2, cols, cz)
    rows = (2 * cols // ngx, cols // ngx)
    steps = 2 + 3 * PARTS
    x_out, grad = pl.pallas_call(
        functools.partial(kernel, (ngx, ngy, nsrc, cx, cy, cols)),
        out_shape=(
            jax.ShapeDtypeStruct((cx, cy, cols, cz), F32),
            jax.ShapeDtypeStruct((cx, cy, cz // nsrc), F32),
        ),
        in_specs=[pl.BlockSpec(memory_space=pltpu.HBM)] * 5,
        out_specs=(pl.BlockSpec(memory_space=pltpu.VMEM),) * 2,
        scratch_shapes=[
            pltpu.VMEM((cx + 2, cy + 2, cols + 8, cz), F32),
            pltpu.VMEM(full, F32),
            pltpu.VMEM(full, F32),
            pltpu.VMEM(full, F32),
            pltpu.VMEM((cx, cy, cols, cz), F32),
            pltpu.VMEM((cx, cy, 7, 8, cz), F32),
            pltpu.VMEM((cx, cy, cz), F32),
            pltpu.VMEM((2, pairs), jnp.int32),
            pltpu.VMEM((1, cols), jnp.int32),
            pltpu.VMEM((2, cols, cz), jnp.int32),
            [pltpu.VMEM((ngx, n, 2 * cols), F32) for n in rows],
            [pltpu.VMEM((ngx - 1, n, 2 * cols), F32) for n in rows],
            [pltpu.VMEM((ngy, n, 2 * cols), F32) for n in rows],
            [pltpu.VMEM((ngx, n, 2 * cols), F32) for n in rows],
            pltpu.VMEM((cx, cy, cz), F32),
            pltpu.VMEM((nsrc - 1, cx, cy, cz), F32),
            dma((steps, 4)), dma((steps, 4)), dma((4 + PARTS,)),
            dma((2, ngx - 1)), dma((2, ngx - 1)),
            dma((2, ngy - 1)), dma((2, ngy - 1)),
            dma((2, ngx - 1)), dma((2, ngx - 1)),
            dma((nsrc - 1,)), dma((nsrc - 1,)),
        ],
        compiler_params=pltpu.CompilerParams(
            collective_id=0, has_side_effects=True, vmem_limit_bytes=32 * 1024 * 1024
        ),
        cost_estimate=pl.CostEstimate(
            flops=4 * 10**8, bytes_accessed=2 * 10**6, transcendentals=0
        ),
    )(
        *[
            pltpu.with_memory_space_constraint(value, pltpu.HBM)
            for value in (
                conductivity, electrodes.T, pair_order.reshape(1, cols),
                initial_fields, adjoint_fields,
            )
        ]
    )
    return x_out.transpose(2, 0, 1, 3), grad


def solution(mesh):
    sizes = (mesh.shape["gx"], mesh.shape["gy"], mesh.shape["src"])
    field = P("src", "gx", "gy", None)
    return jax.shard_map(
        functools.partial(on_device, sizes),
        mesh=mesh,
        in_specs=(P("gx", "gy", None), P(), P("src"), field, field),
        out_specs=(field, P("gx", "gy", "src")),
        check_vma=False,
    )
```
